256 devices in a mesh: req: 64 (over x_hi, z, y), own: 4 (over x_lo, core).
Axes of the slice: x: 4 (x_hi: 2, x_lo: 2; x = x_hi * 2 + x_lo), y: 4, z: 8, core: 2. Of those that a mesh axis runs over, the one named last changes fastest.
Arguments:
- tokens: bfloat16 [32768, 16384], P('req', 'own'), may hold values from -600 to 600
- gain: float32 [16384], replicated, may hold values from 0.1 to 1.9
- gate_weight: bfloat16 [16384, 1024], P('req', 'own'), may hold values from -0.046875 to 0.046875
- up_weight: bfloat16 [16384, 1024], P('req', 'own'), may hold values from -0.046875 to 0.046875
- lengths: int32 [256], P('req'), may hold values from 1 to 128, as said below
- dest: int32 [32768], P('req'), may hold values from 0 to 63, as said below
- owner: int32 [4], replicated, may hold values from 0 to 3, each once
Outputs:
- packed_hidden: bfloat16 [16384, 1024], P('req', 'own')
- hidden_rows: bfloat16 [32768, 1024], P('req', 'own')
The draws below stay inside these ranges and needn't reach their ends.
Inputs may be any that keep to these rules, and one draw needn't show every extreme that they name: `lengths`: each request has 1 to 128 live slots; the live slots of one shard (one index of req) number at most 256, and in every draw some shard has exactly that many. `dest`: counting only live slots, at most 4 slots of one shard name the same shard, and this bound is reached in every draw. Values at slots that are not live are arbitrary.
All inputs are finite; a program needn't handle non-finite values.
Results may differ from the reference program's by a relative error of at most 0.0058.
Values may be sent and summed in bfloat16 or wider, within the bound.
A program may use at most 128 MiB of HBM per device.

```python
import jax
import jax.numpy as jnp
from jax import lax

D = 16384
HID_DEV = 256
TOK_DEV = 512
REQ_DEV = 4
SLOT = 128
PAIR = 4
TOKENS = 32768
H = 1024
N_REQ = 64
N_OWN = 4


def layout_tables(key):
    k_total, k_full, k_move, k_perm, k_dead, k_which = jax.random.split(key, 6)
    top = PAIR * N_REQ
    low = max(4, top // 4)
    totals = jax.random.randint(k_total, (N_REQ,), low, top + 1)
    fullest = jax.random.randint(k_full, (), 0, N_REQ)
    totals = jnp.where(jnp.arange(N_REQ) == fullest, top, totals)
    base = totals // REQ_DEV
    extra = totals % REQ_DEV
    lens = base[:, None] + (jnp.arange(REQ_DEV)[None, :] < extra[:, None]).astype(jnp.int32)
    first = lens[:, 0::2]
    second = lens[:, 1::2]
    lower = jnp.maximum(1 - first, second - SLOT)
    upper = jnp.minimum(SLOT - first, second - 1)
    moved = jax.random.randint(k_move, first.shape, lower, upper + 1)
    first = first + moved
    second = second - moved
    lens = jnp.stack([first, second], axis=2).reshape(N_REQ, REQ_DEV).astype(jnp.int32)
    which = jax.random.randint(k_which, (), 0, REQ_DEV)
    others = REQ_DEV - 1
    rest = top - SLOT
    request_ids = jnp.arange(REQ_DEV, dtype=jnp.int32)
    other_rank = (request_ids - which - 1) % REQ_DEV
    spread_lens = rest // others + (other_rank < rest % others).astype(jnp.int32)
    full_row = jnp.where(request_ids == which, SLOT, spread_lens).astype(jnp.int32)
    lens = jnp.where((jnp.arange(N_REQ) == fullest)[:, None], full_row[None, :], lens).astype(jnp.int32)
    slot = jnp.arange(TOK_DEV)
    request = slot // SLOT
    offset = slot % SLOT
    starts = jnp.cumsum(lens, axis=1) - lens
    order = starts[:, request] + offset[None, :]
    perms = jax.vmap(lambda k: jax.random.permutation(k, N_REQ))(jax.random.split(k_perm, N_REQ))
    live_dest = jnp.take_along_axis(perms, order % N_REQ, axis=1)
    dead_dest = jax.random.randint(k_dead, (N_REQ, TOK_DEV), 0, N_REQ)
    live = offset[None, :] < lens[:, request]
    dest = jnp.where(live, live_dest, dead_dest).astype(jnp.int32)
    return (lens, dest)


def draw_lengths(key, part):
    lens, dest = layout_tables(key)
    return lens.reshape(-1).astype(jnp.int32)


def draw_dest(key, part):
    lens, dest = layout_tables(key)
    return dest.reshape(-1).astype(jnp.int32)


def draw_tokens(key, part):
    key = jax.random.fold_in(key, 11)
    k_rows, k_cols, k_base = jax.random.split(key, 3)
    rows = jnp.exp(jax.random.uniform(k_rows, (TOKENS, 1), jnp.float32) * jnp.log(10.0))
    cols = jnp.exp(jax.random.uniform(k_cols, (1, D), jnp.float32) * jnp.log(10.0))
    base = jnp.clip(jax.random.normal(k_base, (TOKENS, D), jnp.float32), -6.0, 6.0)
    return (base * rows * cols).astype(jnp.bfloat16)


def levels(rng, extent, cuts, smallest, largest):
    factor_of, own = 1.0, jax.random.fold_in(rng, 6)
    for axis_at, blocks in cuts:
        steps = jnp.exp(jax.random.uniform(jax.random.fold_in(own, axis_at), (blocks,), jnp.float32, smallest / len(cuts), largest / len(cuts)))
        factor_of = factor_of * jnp.repeat(steps, extent[axis_at] // blocks).reshape([-1 if axis == axis_at else 1 for axis in range(len(extent))])
    return factor_of


def centred(key, dims, deviation, most, cuts=(), kind=jnp.bfloat16):
    loudness = levels(key, dims, cuts, -0.22, 0.18) if cuts else 1.0
    drawn = jax.random.normal(key, dims, jnp.float32) * deviation * loudness
    return jnp.minimum(jnp.maximum(drawn, -most), most).astype(kind)


def setup_inputs(seed: int = 0) -> dict:
    splits = jax.random.split(jax.random.key(seed), 8)
    tokens = draw_tokens(jax.random.fold_in(splits[7], 71), 0)
    gain = jnp.clip(1.0 + 0.18 * jax.random.normal(splits[1], (D,), jnp.float32), 0.1, 1.9)
    gate_weight = centred(splits[2], (D, H), D ** -0.5, 0.046875, ((0, 64), (1, 4)))
    up_weight = centred(splits[3], (D, H), D ** -0.5, 0.046875, ((0, 64), (1, 4)))
    lengths = draw_lengths(jax.random.fold_in(splits[7], 71), 0)
    dest = draw_dest(jax.random.fold_in(splits[7], 71), 0)
    owner = jax.random.permutation(splits[6], N_OWN).astype(jnp.int32)
    return {"tokens": tokens, "gain": gain, "gate_weight": gate_weight, "up_weight": up_weight, "lengths": lengths, "dest": dest, "owner": owner}


norm_eps = 1e-05

def rms_rows(rows, gain):
    wide = rows.astype(jnp.float32)
    scale = lax.rsqrt(lax.optimization_barrier(jnp.mean(wide * wide, axis=-1, keepdims=True)) + norm_eps)
    return (wide * scale * gain).astype(jnp.bfloat16)

def reference(tokens, gain, gate_weight, up_weight, lengths, dest, owner):
    slots = N_REQ * PAIR
    total = N_REQ * slots
    position = jnp.arange(TOKENS, dtype=jnp.int32)
    shard = position // TOK_DEV
    within = position % TOK_DEV
    live = within % SLOT < lengths[(shard * REQ_DEV + within // SLOT).astype(jnp.int32)]
    marks = ((dest[:, None] == jnp.arange(N_REQ, dtype=jnp.int32)[None, :]) & live[:, None]).astype(jnp.int32)
    grouped = marks.reshape(N_REQ, TOK_DEV, N_REQ)
    before = (jnp.cumsum(grouped, axis=1) - grouped).reshape(TOKENS, N_REQ)
    rank = lax.optimization_barrier(jnp.sum(before * marks, axis=1)).astype(jnp.int32)
    place = jnp.where(live, dest * slots + shard * PAIR + rank, total).astype(jnp.int32)
    source = jnp.zeros((total,), jnp.int32).at[place].set(position, mode='drop')
    filled = jnp.zeros((total,), bool).at[place].set(True, mode='drop')
    inverse = jnp.zeros((N_OWN,), jnp.int32).at[owner].set(jnp.arange(N_OWN, dtype=jnp.int32))
    up_panel = up_weight.reshape(D, N_OWN, HID_DEV)[:, inverse, :].reshape(D, H)

    def one_shard(block):
        index, valid = block
        rows = jnp.where(valid[:, None], tokens[index], 0)
        normed = rms_rows(rows, gain)
        gate = jnp.dot(normed, gate_weight, preferred_element_type=jnp.float32)
        up = jnp.dot(normed, up_panel, preferred_element_type=jnp.float32)
        return (jax.nn.silu(gate) * up).astype(jnp.bfloat16)
    packed = lax.map(one_shard, (source.reshape(N_REQ, slots), filled.reshape(N_REQ, slots))).reshape(total, H)
    picked = packed[jnp.minimum(place, total - 1)]
    hidden_rows = jnp.where(live[:, None], picked, 0).astype(jnp.bfloat16)
    return (packed, hidden_rows)
```

```python
import functools

import jax
import jax.numpy as jnp
from jax import lax
from jax.experimental import pallas as pl
from jax.experimental.pallas import tpu as pltpu
from jax.sharding import PartitionSpec as P

MESH = pl.DeviceIdType.MESH
f32 = jnp.float32
bf16 = jnp.bfloat16

norm_eps = 1e-05
D = 16384
N_REQ = 64
N_OWN = 4
NX, NY, NZ = 4, 4, 8
TOK = 512
ROWS = 256
HID = 256
FEAT = 4096
PAIR = 4
SUB = 1
NQ = N_OWN * SUB
HC = HID // SUB
WC = 2 * HC
CUT = 144
STREAM = 5 * NQ
HOP, RING_ON, RING_END, AHEAD, JOIN = 2, 2, 4, 4, 2
LAST = 4 * HOP + max(4, RING_END)


def kernel(
    gain, owner, lengths, dest, tok_hbm, gate_w, up_w,
    packed_out, local_out,
    tok, pick, act, act_out, panel, root_gate, root_up, squares, squares_in,
    part, part_in, red_out, red_in, hid, a2a_out, a2a_in, wide,
    s_tok, s_act, s_root_out, s_gate_in, s_up_in, s_sq_out, s_sq_in,
    s_chain_out, s_chain_in, s_ring_out, s_ring_in, s_edge_out, s_edge_in, s_spread_out, s_spread_in,
    s_part_out, s_part_in, s_red_out, s_red_in, s_a2a_out, s_a2a_in,
):
    req = lax.axis_index("req")
    own = lax.axis_index("own")
    h, z, y = req // 32, (req // 4) % 8, req % 4
    j, c = own // 2, own % 2
    x = 2 * h + j

    def at(x_, y_, z_, c_):
        x_, y_, z_ = lax.rem(x_ + NX, NX), lax.rem(y_ + NY, NY), lax.rem(z_ + NZ, NZ)
        return ((x_ // 2 * NZ + z_) * NY + y_, (x_ % 2) * 2 + c_)

    def remote(src, dst, send, recv, device):
        return pltpu.make_async_remote_copy(
            src_ref=src, dst_ref=dst, send_sem=send, recv_sem=recv, device_id=device, device_id_type=MESH
        )

    def arrived(ref, sem):
        pltpu.make_async_copy(ref, ref, sem).wait()


    barrier = pltpu.get_barrier_semaphore()

    def greet_req(i, _):
        pl.semaphore_signal(barrier, inc=1, device_id=(lax.rem(req + i, N_REQ), own), device_id_type=MESH)
        return 0

    lax.fori_loop(1, N_REQ, greet_req, 0)
    for k in range(1, N_OWN):
        peer = lax.rem(own + k, N_OWN)
        for other in (req, lax.rem(req + 32, N_REQ)):
            pl.semaphore_signal(barrier, inc=1, device_id=(other, peer), device_id_type=MESH)

    fetch = pltpu.make_async_copy(tok_hbm, tok, s_tok)
    fetch.start()

    slot = lax.broadcasted_iota(jnp.int32, (1, TOK), 1)
    span = jnp.where(
        slot < 128, lengths[0], jnp.where(slot < 256, lengths[1], jnp.where(slot < 384, lengths[2], lengths[3]))
    )
    live = (slot % 128) < span
    to = jnp.where(live, dest[...], -1)
    marks = (lax.broadcasted_iota(jnp.int32, (N_REQ, TOK), 0) == to).astype(f32)
    earlier = lax.broadcasted_iota(jnp.int32, (TOK, TOK), 0) < lax.broadcasted_iota(jnp.int32, (TOK, TOK), 1)
    before = jnp.dot(marks.astype(bf16), earlier.astype(f32).astype(bf16), preferred_element_type=f32)
    rank = jnp.sum(before * marks, axis=0, keepdims=True)
    row = jnp.where(live, rank * N_REQ + to.astype(f32), -1.0)
    pick[...] = (lax.broadcasted_iota(jnp.int32, (ROWS, TOK), 0).astype(f32) == row).astype(f32).astype(bf16)
    fetch.wait()

    mine = pl.ds(pl.multiple_of(h * ROWS, ROWS), ROWS)

    def arrange(block, out):
        col = pl.multiple_of(block * 1024, 1024)
        rows = jnp.dot(pick[...], tok[:, pl.ds(col, 1024)], preferred_element_type=f32)
        sq = rows * rows
        for k in range(8):
            squares[...] += sq[:, k * 128 : (k + 1) * 128]
        scaled = rows * gain[:, pl.ds(pl.multiple_of(own * FEAT + block * 1024, 1024), 1024)]
        out[...] = scaled.astype(bf16)

    squares[...] = jnp.zeros_like(squares)
    for zz in range(2):
        arrange(1 - h + 2 * zz, act_out.at[:, pl.ds(zz * 1024, 1024)])

    pl.semaphore_wait(barrier, N_REQ - 1 + 2 * (N_OWN - 1))

    root = at(2 * (z % 2) + h, y, z, z // 4)
    self_root = jnp.logical_and(2 * (z % 2) + h == x, z // 4 == c)

    @pl.when(self_root)
    def _():
        pltpu.make_async_copy(up_w, root_up.at[own], s_up_in.at[own]).start()
        pltpu.make_async_copy(gate_w, root_gate.at[own], s_gate_in.at[own]).start()

    @pl.when(jnp.logical_not(self_root))
    def _():
        remote(up_w, root_up.at[own], s_root_out.at[0], s_up_in.at[own], root).start()
        remote(gate_w, root_gate.at[own], s_root_out.at[1], s_gate_in.at[own], root).start()

    partner = (lax.rem(req + 32, N_REQ), own)
    give = remote(act_out, act.at[mine], s_act.at[0], s_act.at[1], partner)
    give.start()

    for zz in range(2):
        arrange(h + 2 * zz, act.at[mine, pl.ds(zz * 1024, 1024)])
    sq_sends = []
    for k in range(1, N_OWN):
        peer = lax.rem(own + k, N_OWN)
        cp = remote(squares, squares_in.at[k - 1], s_sq_out.at[k - 1], s_sq_in.at[k - 1], (req, peer))
        cp.start()
        sq_sends.append(cp)

    is_root = jnp.logical_and(z % 2 == h, z // 4 == c)
    zr = (z % 4) // 2

    def block(q, zz, yy, rows):
        return panel.at[q, zz, yy, pl.ds(rows[0], rows[1])]

    ra, rb = (0, CUT), (CUT, ROWS - CUT)

    def z_next(way):
        return at(x, y, z + 1 - 2 * way, c)

    def chain_copy(q, zz, way):
        ref = block(q, zz, y, ra)
        return remote(ref, ref, s_chain_out.at[q, zz, way], s_chain_in.at[q, zz], z_next(way))

    def spread_copy(q, zz, k, way):
        ref = block(q, zz, lax.rem(y + k, NY), rb)
        return remote(ref, ref, s_spread_out.at[q, zz, k, way], s_spread_in.at[q, zz, k], z_next(way))

    def y_copy(q, zz, k, rows, out, into, turn):
        way = turn if k == 2 else k
        yy = lax.rem(y + 3 - 2 * way, NY) if k == 2 else y
        ref = block(q, zz, yy, rows)
        return remote(ref, ref, out, into, at(x, y + 1 - 2 * way, z, c))

    def ring_copy(q, zz, k):
        return y_copy(q, zz, k, ra, s_ring_out.at[q, zz, k], s_ring_in.at[q, zz, k], zz)

    def edge_copy(q, k):
        return y_copy(q, zr, k, rb, s_edge_out.at[q, k], s_edge_in.at[q, k], lax.rem(q, 2))

    def y_arrived(q, zz, k, rows, into, turn):
        step = 2 if k == 2 else 3 - 2 * k
        arrived(block(q, zz, lax.rem(y + step, NY), rows), into)

    def reach(q, zz):
        d = lax.rem(z - (4 * c + h + 2 * zz) + 2 * NZ, NZ)
        far = 4 - lax.rem(q + zz, 2)
        return d, jnp.logical_and(d > 0, d < far), d >= far + 2

    def hops(zz):
        d = lax.rem(z - (4 * c + h + 2 * zz) + 2 * NZ, NZ)
        return jnp.minimum(d, NZ - d)

    def load_panel(q):
        @pl.when(q == 0)
        def _():
            for k in range(N_OWN):
                arrived(root_up.at[k], s_up_in.at[k])

        o, s = q // SUB, lax.rem(q, SUB)

        @pl.when(s == 0)
        def _():
            arrived(root_gate.at[o], s_gate_in.at[o])

        stored = jnp.int32(0)
        for k in range(1, N_OWN):
            stored = jnp.where(owner[k] == o, k, stored)
        cols = pl.ds(pl.multiple_of(s * HC, HC), HC)
        panel[q, zr, y, :, :HC] = root_gate[o, :, cols]
        panel[q, zr, y, :, HC:] = root_up[stored, :, cols]

    def open_edges(q):
        load_panel(q)
        for k in range(2):
            edge_copy(q, k).start()

    def on_chain(q, zz):
        d, up, down = reach(q, zz)

        @pl.when(d == 0)
        def _():
            @pl.when(q == 0)
            def _():
                open_edges(q)

            for way in range(2):
                chain_copy(q, zz, way).start()

        @pl.when(d > 0)
        def _():
            arrived(block(q, zz, y, ra), s_chain_in.at[q, zz])

            @pl.when(jnp.logical_or(up, down))
            def _():
                chain_copy(q, zz, down.astype(jnp.int32)).start()

        for k in range(2):
            ring_copy(q, zz, k).start()

    def on_spread(q, zz, i):
        k = jnp.where(i == 1, 0, jnp.where(i == 2, 3, jnp.where(i == 3, 1, 2)))
        d, up, down = reach(q, zz)

        @pl.when(d == 0)
        def _():
            @pl.when(i > 1)
            def _():
                arrived(block(q, zz, lax.rem(y + k, NY), rb), s_edge_in.at[q, i - 2])

                @pl.when(i == 2 + lax.rem(q, 2))
                def _():
                    edge_copy(q, 2).start()

            for way in range(2):
                spread_copy(q, zz, k, way).start()

            @pl.when(jnp.logical_and(i == AHEAD, q < NQ - 1))
            def _():
                open_edges(q + 1)

        @pl.when(d > 0)
        def _():
            arrived(block(q, zz, lax.rem(y + k, NY), rb), s_spread_in.at[q, zz, k])

            @pl.when(jnp.logical_or(up, down))
            def _():
                spread_copy(q, zz, k, down.astype(jnp.int32)).start()

    def flow(n, zz):
        @pl.when(jnp.logical_and(n >= 0, n < STREAM))
        def _():
            q = n // 5
            i = n - 5 * q

            @pl.when(i == 0)
            def _():
                on_chain(q, zz)

            @pl.when(i > 0)
            def _():
                on_spread(q, zz, i)

    def each_chunk(n, f):
        @pl.when(jnp.logical_and(jnp.logical_and(n >= 0, n < STREAM), lax.rem(n + 5 * 64, 5) == 0))
        def _():
            f(n // 5)

    def ring_on(zz, q):
        y_arrived(q, zz, zz, ra, s_ring_in.at[q, zz, zz], zz)
        ring_copy(q, zz, 2).start()

    def ring_end(zz, q):
        y_arrived(q, zz, 1 - zz, ra, s_ring_in.at[q, zz, 1 - zz], zz)
        y_arrived(q, zz, 2, ra, s_ring_in.at[q, zz, 2], zz)

    keep = pl.ds(pl.multiple_of(c * ROWS, ROWS), ROWS)
    pass_on = pl.ds(pl.multiple_of((1 - c) * ROWS, ROWS), ROWS)

    def part_copy(q):
        return remote(part.at[q, pass_on], part_in.at[q], s_part_out.at[q], s_part_in.at[q], (req, 2 * j + 1 - c))

    def dot(q):
        @pl.when(q == 0)
        def _():
            give.wait_recv()

        w = panel[q].reshape(8 * ROWS, WC)
        part[q] = jnp.dot(act[...], w, preferred_element_type=f32)
        part_copy(q).start()

    def red_to(q):
        o = q // SUB
        there = 2 * c + o // 2
        return at(there, y, z, o % 2), jnp.logical_and(there == x, o % 2 == c)

    def red_copy(q):
        device, _ = red_to(q)
        return remote(red_out.at[q], red_in.at[x, q % SUB], s_red_out.at[q], s_red_in.at[x, q % SUB], device)

    def total(q):
        arrived(part_in.at[q], s_part_in.at[q])
        _, here = red_to(q)
        both = (part[q, keep] + part_in[q]).astype(bf16)

        @pl.when(here)
        def _():
            red_in[x, q % SUB] = both

        @pl.when(jnp.logical_not(here))
        def _():
            red_out[q] = both
            red_copy(q).start()

    first = (hops(1) < hops(0)).astype(jnp.int32)

    def turn(t, _):
        for zz in (first, 1 - first):
            flow(t - HOP * hops(zz), zz)
        for zz in range(2):
            each_chunk(t - HOP * hops(zz) - RING_ON, functools.partial(ring_on, zz))
        for zz in range(2):
            each_chunk(t - HOP * hops(zz) - RING_END, functools.partial(ring_end, zz))
        each_chunk(t - LAST, dot)
        each_chunk(t - LAST - JOIN, total)
        return 0

    lax.fori_loop(0, STREAM - 4 + LAST + JOIN, turn, 0)

    for k in range(N_OWN - 1):
        arrived(squares_in.at[k], s_sq_in.at[k])
    sq = squares[...] + squares_in[0] + squares_in[1] + squares_in[2]
    scale = lax.rsqrt(jnp.sum(sq, axis=1, keepdims=True) * (1.0 / D) + norm_eps)

    for k in range(NX):
        @pl.when(jnp.logical_or(x != k, h != c))
        def _():
            for s in range(SUB):
                arrived(red_in.at[k, s], s_red_in.at[k, s])

    for s in range(SUB):
        both = red_in[0, s].astype(f32)
        for k in range(1, NX):
            both = both + red_in[k, s].astype(f32)
        gate = both[:, :HC] * scale
        up = both[:, HC:] * scale
        hid[:, s * HC : (s + 1) * HC] = (gate / (1.0 + jnp.exp(-gate)) * up).astype(bf16)

    for half in range(2):
        wide[...] = hid[:, half * 128 : (half + 1) * 128].astype(f32)
        for k in range(PAIR):
            a2a_out[pl.ds(half * PAIR + k, N_REQ, stride=8), :] = wide[k * N_REQ : (k + 1) * N_REQ, :]

    my_tile = pl.ds(pl.multiple_of(req * 8, 8), 8)

    def send_tile(i, _):
        to_req = lax.rem(req + i, N_REQ)
        src = a2a_out.at[pl.ds(pl.multiple_of(to_req * 8, 8), 8)]
        remote(src, a2a_in.at[my_tile], s_a2a_out, s_a2a_in, (to_req, own)).start()
        return 0

    lax.fori_loop(1, N_REQ, send_tile, 0)
    local_out[...] = lax.dot_general(
        pick[...], hid[...], (((0,), (0,)), ((), ())), preferred_element_type=f32
    ).astype(bf16)
    a2a_in[my_tile, :] = a2a_out[my_tile, :]

    def drain(q, _):
        for zz in range(2):
            d, up, down = reach(q, zz)
            for way, on in enumerate((up, down)):
                @pl.when(jnp.logical_or(d == 0, on))
                def _():
                    chain_copy(q, zz, way).wait_send()
                    for k in range(NY):
                        spread_copy(q, zz, k, way).wait_send()
            for k in range(3):
                ring_copy(q, zz, k).wait_send()

        @pl.when(is_root)
        def _():
            for k in range(3):
                edge_copy(q, k).wait_send()

        part_copy(q).wait_send()
        _, here = red_to(q)

        @pl.when(jnp.logical_not(here))
        def _():
            red_copy(q).wait_send()
        return 0

    lax.fori_loop(0, NQ, drain, 0)
    give.wait_send()
    for cp in sq_sends:
        cp.wait_send()

    @pl.when(jnp.logical_not(self_root))
    def _():
        remote(up_w, root_up.at[own], s_root_out.at[0], s_up_in.at[own], root).wait_send()
        remote(gate_w, root_gate.at[own], s_root_out.at[1], s_gate_in.at[own], root).wait_send()

    others = pl.ds(0, 8 * (N_REQ - 1))
    arrived(a2a_out.at[others], s_a2a_out)
    arrived(a2a_in.at[others], s_a2a_in)
    for half in range(2):
        for k in range(PAIR):
            wide[pl.ds(k, N_REQ, stride=PAIR), :] = a2a_in[pl.ds(half * PAIR + k, N_REQ, stride=8), :]
        packed_out[:, half * 128 : (half + 1) * 128] = wide[...].astype(bf16)


def body(tokens, gain, gate_weight, up_weight, lengths, dest, owner):
    vmem = pl.BlockSpec(memory_space=pltpu.VMEM)
    smem = pl.BlockSpec(memory_space=pltpu.SMEM)
    dma = pltpu.SemaphoreType.DMA
    return pl.pallas_call(
        kernel,
        out_shape=(jax.ShapeDtypeStruct((ROWS, HID), bf16), jax.ShapeDtypeStruct((TOK, HID), bf16)),
        in_specs=[vmem, smem, smem, vmem, pl.BlockSpec(memory_space=pl.ANY), vmem, vmem],
        out_specs=(vmem, vmem),
        scratch_shapes=[
            pltpu.VMEM((TOK, FEAT), bf16),
            pltpu.VMEM((ROWS, TOK), bf16),
            pltpu.VMEM((2 * ROWS, FEAT // 2), bf16),
            pltpu.VMEM((ROWS, FEAT // 2), bf16),
            pltpu.VMEM((NQ, 2, NY, ROWS, WC), bf16),
            pltpu.VMEM((N_OWN, ROWS, HID), bf16),
            pltpu.VMEM((N_OWN, ROWS, HID), bf16),
            pltpu.VMEM((ROWS, 128), f32),
            pltpu.VMEM((N_OWN - 1, ROWS, 128), f32),
            pltpu.VMEM((NQ, 2 * ROWS, WC), f32),
            pltpu.VMEM((NQ, ROWS, WC), f32),
            pltpu.VMEM((NQ, ROWS, WC), bf16),
            pltpu.VMEM((NX, SUB, ROWS, WC), bf16),
            pltpu.VMEM((ROWS, HID), bf16),
            pltpu.VMEM((8 * N_REQ, 128), f32),
            pltpu.VMEM((8 * N_REQ, 128), f32),
            pltpu.VMEM((ROWS, 128), f32),
            dma, dma((2,)), dma((2,)), dma((N_OWN,)), dma((N_OWN,)), dma((N_OWN - 1,)), dma((N_OWN - 1,)),
            dma((NQ, 2, 2)), dma((NQ, 2)), dma((NQ, 2, 3)), dma((NQ, 2, 3)), dma((NQ, 3)), dma((NQ, 3)),
            dma((NQ, 2, NY, 2)), dma((NQ, 2, NY)),
            dma((NQ,)), dma((NQ,)), dma((NQ,)), dma((NX, SUB)), dma, dma,
        ],
        compiler_params=pltpu.CompilerParams(
            collective_id=0, has_side_effects=True, vmem_limit_bytes=56 * 2**20
        ),
        name="swiglu_panel",
    )(gain.reshape(1, D), owner, lengths, dest.reshape(1, TOK), tokens, gate_weight, up_weight)


def solution(mesh):
    placed = (P("req", "own"), P(), P("req", "own"), P("req", "own"), P("req"), P("req"), P())
    return jax.shard_map(
        body,
        mesh=mesh,
        in_specs=placed,
        out_specs=(P("req", "own"), P("req", "own")),
        check_vma=False,
    )
```

```python
import functools

import jax
import jax.numpy as jnp
from jax import lax
from jax.experimental import pallas as pl
from jax.experimental.pallas import tpu as pltpu
from jax.sharding import PartitionSpec as P

MESH = pl.DeviceIdType.MESH
f32 = jnp.float32
bf16 = jnp.bfloat16

norm_eps = 1e-05
D = 16384
N_REQ = 64
N_OWN = 4
NX, NY, NZ = 4, 4, 8
TOK = 512
ROWS = 256
HID = 256
FEAT = 4096
PAIR = 4
NQ = 4
WC = 2 * HID
CUT = 160
STREAM = 5 * NQ
HOP, RING_ON, RING_END, AHEAD, JOIN = 3, 3, 5, 4, 2
GATES_T, UPS_T, GIVE_T, NORM_T, RELAY_T = 1, 2, 5, 7, 2
LAST = 4 * HOP + max(4, RING_END)


def kernel(
    gain, owner, lengths, dest, tok_hbm, gate_w, up_w,
    packed_out, local_hbm,
    tok, pick, act, act_out, panel, root_up, squares, squares_out, squares_in,
    part, part_in, red_out, red_in, hid, local_out, a2a_out, a2a_in, wide,
    s_tok, s_act, s_root_out, s_gate_in, s_up_in, s_sq_out, s_sq_in,
    s_chain_out, s_chain_in, s_ring_out, s_ring_in, s_edge_out, s_edge_in, s_spread_out, s_spread_in,
    s_part_out, s_part_in, s_red_out, s_red_in, s_a2a_out, s_a2a_in, s_local, relay,
):
    req = lax.axis_index("req")
    own = lax.axis_index("own")
    h, z, y = req // 32, (req // 4) % 8, req % 4
    j, c = own // 2, own % 2
    x = 2 * h + j

    def at(x_, y_, z_, c_):
        x_, y_, z_ = lax.rem(x_ + NX, NX), lax.rem(y_ + NY, NY), lax.rem(z_ + NZ, NZ)
        return ((x_ // 2 * NZ + z_) * NY + y_, (x_ % 2) * 2 + c_)

    def remote(src, dst, send, recv, device):
        return pltpu.make_async_remote_copy(
            src_ref=src, dst_ref=dst, send_sem=send, recv_sem=recv, device_id=device, device_id_type=MESH
        )

    def arrived(ref, sem):
        pltpu.make_async_copy(ref, ref, sem).wait()


    barrier = pltpu.get_barrier_semaphore()
    other_req = lax.rem(req + 32, N_REQ)
    beside = [at(x, y + 1, z, c), at(x, y - 1, z, c)], [at(x, y, z + 1, c), at(x, y, z - 1, c)]
    line = [(req, lax.rem(own + k, N_OWN)) for k in range(1, N_OWN)]
    line += [(other_req, lax.rem(own + k, N_OWN)) for k in range(N_OWN)]
    for device in line + beside[0] + beside[1]:
        pl.semaphore_signal(barrier, inc=1, device_id=device, device_id_type=MESH)

    fetch = pltpu.make_async_copy(tok_hbm, tok, s_tok)
    fetch.start()
    pl.semaphore_wait(barrier, 11)

    def pass_word(i):
        if i > 0:
            pl.semaphore_wait(relay.at[i - 1], 2)
        if i < 6:
            for device in beside[0 if i < 2 else 1]:
                pl.semaphore_signal(relay.at[i], inc=1, device_id=device, device_id_type=MESH)

    root = at(2 * (z % 2) + h, y, z, z // 4)
    self_root = jnp.logical_and(2 * (z % 2) + h == x, z // 4 == c)
    is_root = jnp.logical_and(z % 2 == h, z // 4 == c)
    zr = (z % 4) // 2

    def gate_at(k):
        return panel.at[k // 2, zr, y, :, pl.ds(pl.multiple_of(k % 2 * HID, HID), HID)]

    def to_root(src, dst, out, into):
        @pl.when(self_root)
        def _():
            pltpu.make_async_copy(src, dst, into).start()

        @pl.when(jnp.logical_not(self_root))
        def _():
            remote(src, dst, out, into, root).start()

    def gates_to_root():
        to_root(gate_w, gate_at(own), s_root_out.at[0], s_gate_in.at[own])

    def ups_to_root():
        to_root(up_w, root_up.at[own], s_root_out.at[1], s_up_in.at[own])

    gates_to_root()
    ups_to_root()

    pass_word(0)

    slot = lax.broadcasted_iota(jnp.int32, (1, TOK), 1)
    span = jnp.where(
        slot < 128, lengths[0], jnp.where(slot < 256, lengths[1], jnp.where(slot < 384, lengths[2], lengths[3]))
    )
    live = (slot % 128) < span
    to = jnp.where(live, dest[...], -1)
    marks = (lax.broadcasted_iota(jnp.int32, (N_REQ, TOK), 0) == to).astype(f32)
    earlier = lax.broadcasted_iota(jnp.int32, (TOK, TOK), 0) < lax.broadcasted_iota(jnp.int32, (TOK, TOK), 1)
    before = jnp.dot(marks.astype(bf16), earlier.astype(f32).astype(bf16), preferred_element_type=f32)
    rank = jnp.sum(before * marks, axis=0, keepdims=True)
    row = jnp.where(live, rank * N_REQ + to.astype(f32), -1.0)
    pick[...] = (lax.broadcasted_iota(jnp.int32, (ROWS, TOK), 0).astype(f32) == row).astype(f32).astype(bf16)
    fetch.wait()

    mine = pl.ds(pl.multiple_of(h * ROWS, ROWS), ROWS)

    def arrange(block, out):
        col = pl.multiple_of(block * 1024, 1024)
        rows = jnp.dot(pick[...], tok[:, pl.ds(col, 1024)], preferred_element_type=f32)
        sq = rows * rows
        for k in range(8):
            squares[...] += sq[:, k * 128 : (k + 1) * 128]
        out[...] = rows.astype(bf16)

    squares[...] = jnp.zeros_like(squares)
    for zz in range(2):
        arrange(1 - h + 2 * zz, act_out.at[:, pl.ds(zz * 1024, 1024)])
    for zz in range(2):
        arrange(h + 2 * zz, act.at[mine, pl.ds(zz * 1024, 1024)])

    partner = (other_req, own)
    give = remote(act_out, act.at[mine], s_act.at[0], s_act.at[1], partner)

    def turned(a, axis):
        eye = lax.broadcasted_iota(jnp.int32, (ROWS, ROWS), 0) == lax.broadcasted_iota(jnp.int32, (ROWS, ROWS), 1)
        return jnp.sum(jnp.where(eye, a, 0.0), axis=axis, keepdims=True)

    row_sums = turned(jnp.sum(squares[...], axis=1, keepdims=True), 0)
    squares_out[...] = jnp.broadcast_to(row_sums, (8, ROWS))
    sq_sends = []
    for k, device in enumerate(line):
        cp = remote(squares_out, squares_in.at[2 * own + h], s_sq_out.at[k], s_sq_in.at[2 * own + h], device)
        cp.start()
        sq_sends.append(cp)
    squares_in[2 * own + h] = squares_out[...]

    def normalize(hh):
        sums = squares_in[hh, 0:1, :]
        for k in range(1, N_OWN):
            sums = sums + squares_in[2 * k + hh, 0:1, :]
        scale = lax.rsqrt(turned(sums, 1) * (1.0 / D) + norm_eps)
        rows = pl.ds(pl.multiple_of(hh * ROWS, ROWS), ROWS)
        for zz in range(2):
            for n in range(2):
                cols = pl.ds(zz * 1024 + n * 512, 512)
                here = pl.multiple_of(own * FEAT + (h + 2 * zz) * 1024 + n * 512, 512)
                act[rows, cols] = (act[rows, cols].astype(f32) * scale * gain[:, pl.ds(here, 512)]).astype(bf16)

    def block(q, zz, yy, rows):
        return panel.at[q, zz, yy, pl.ds(rows[0], rows[1])]

    ra, rb = (0, CUT), (CUT, ROWS - CUT)

    def z_next(way):
        return at(x, y, z + 1 - 2 * way, c)

    def chain_copy(q, zz, way):
        ref = block(q, zz, y, ra)
        return remote(ref, ref, s_chain_out.at[q, zz, way], s_chain_in.at[q, zz], z_next(way))

    def spread_copy(q, zz, k, way):
        ref = block(q, zz, lax.rem(y + k, NY), rb)
        return remote(ref, ref, s_spread_out.at[q, zz, k, way], s_spread_in.at[q, zz, k], z_next(way))

    def y_copy(q, zz, k, rows, out, into, turn):
        way = turn if k == 2 else k
        yy = lax.rem(y + 3 - 2 * way, NY) if k == 2 else y
        ref = block(q, zz, yy, rows)
        return remote(ref, ref, out, into, at(x, y + 1 - 2 * way, z, c))

    def ring_copy(q, zz, k):
        return y_copy(q, zz, k, ra, s_ring_out.at[q, zz, k], s_ring_in.at[q, zz, k], zz)

    def edge_copy(q, k):
        return y_copy(q, zr, k, rb, s_edge_out.at[q, k], s_edge_in.at[q, k], lax.rem(q, 2))

    def y_arrived(q, zz, k, rows, into, turn):
        step = 2 if k == 2 else 3 - 2 * k
        arrived(block(q, zz, lax.rem(y + step, NY), rows), into)

    def reach(q, zz):
        d = lax.rem(z - (4 * c + h + 2 * zz) + 2 * NZ, NZ)
        far = 4 - lax.rem(q + zz, 2)
        return d, jnp.logical_and(d > 0, d < far), d >= far + 2

    def hops(zz):
        d = lax.rem(z - (4 * c + h + 2 * zz) + 2 * NZ, NZ)
        return jnp.minimum(d, NZ - d)

    def load_panel(q):
        @pl.when(q < 2)
        def _():
            for k in range(2):
                arrived(gate_at(2 * q + k), s_gate_in.at[2 * q + k])

        @pl.when(q == 2)
        def _():
            for k in range(N_OWN):
                arrived(root_up.at[k], s_up_in.at[k])

        @pl.when(q >= 2)
        def _():
            for k in range(2):
                stored = jnp.int32(0)
                for m in range(1, N_OWN):
                    stored = jnp.where(owner[m] == 2 * (q - 2) + k, m, stored)
                panel[q, zr, y, :, k * HID : (k + 1) * HID] = root_up[stored]

    def open_edges(q):
        load_panel(q)
        for k in range(2):
            edge_copy(q, k).start()

    def on_chain(q, zz):
        d, up, down = reach(q, zz)

        @pl.when(d == 0)
        def _():
            @pl.when(q == 0)
            def _():
                open_edges(q)

            for way in range(2):
                chain_copy(q, zz, way).start()

        @pl.when(d > 0)
        def _():
            arrived(block(q, zz, y, ra), s_chain_in.at[q, zz])

            @pl.when(jnp.logical_or(up, down))
            def _():
                chain_copy(q, zz, down.astype(jnp.int32)).start()

        for k in range(2):
            ring_copy(q, zz, k).start()

    def on_spread(q, zz, i):
        k = jnp.where(i == 1, 0, jnp.where(i == 2, 3, jnp.where(i == 3, 1, 2)))
        d, up, down = reach(q, zz)

        @pl.when(d == 0)
        def _():
            @pl.when(i > 1)
            def _():
                arrived(block(q, zz, lax.rem(y + k, NY), rb), s_edge_in.at[q, i - 2])

                @pl.when(i == 2 + lax.rem(q, 2))
                def _():
                    edge_copy(q, 2).start()

            for way in range(2):
                spread_copy(q, zz, k, way).start()

            @pl.when(jnp.logical_and(i == AHEAD, q < NQ - 1))
            def _():
                open_edges(q + 1)

        @pl.when(d > 0)
        def _():
            arrived(block(q, zz, lax.rem(y + k, NY), rb), s_spread_in.at[q, zz, k])

            @pl.when(jnp.logical_or(up, down))
            def _():
                spread_copy(q, zz, k, down.astype(jnp.int32)).start()

    def flow(n, zz):
        @pl.when(jnp.logical_and(n >= 0, n < STREAM))
        def _():
            q = n // 5
            i = n - 5 * q

            @pl.when(i == 0)
            def _():
                on_chain(q, zz)

            @pl.when(i > 0)
            def _():
                on_spread(q, zz, i)

    def each_chunk(n, f):
        @pl.when(jnp.logical_and(jnp.logical_and(n >= 0, n < STREAM), lax.rem(n + 5 * 64, 5) == 0))
        def _():
            f(n // 5)

    def ring_on(zz, q):
        y_arrived(q, zz, zz, ra, s_ring_in.at[q, zz, zz], zz)
        ring_copy(q, zz, 2).start()

    def ring_end(zz, q):
        y_arrived(q, zz, 1 - zz, ra, s_ring_in.at[q, zz, 1 - zz], zz)
        y_arrived(q, zz, 2, ra, s_ring_in.at[q, zz, 2], zz)

    keep = pl.ds(pl.multiple_of(c * ROWS, ROWS), ROWS)
    pass_on = pl.ds(pl.multiple_of((1 - c) * ROWS, ROWS), ROWS)

    def part_copy(q, k):
        return remote(
            part.at[q, k, pass_on], part_in.at[q, k], s_part_out.at[q, k], s_part_in.at[q, k], (req, 2 * j + 1 - c)
        )

    def dot(q):
        for k in range(2):
            w = panel[q, :, :, :, k * HID : (k + 1) * HID].reshape(8 * ROWS, HID)
            part[q, k] = jnp.dot(act[...], w, preferred_element_type=f32)
            part_copy(q, k).start()

    def red_copy(q, k):
        device = at(2 * c + lax.rem(q, 2), y, z, k)
        return remote(red_out.at[q, k], red_in.at[x, q // 2], s_red_out.at[q, k], s_red_in.at[x, q // 2], device)

    def red_here(q, k):
        return jnp.logical_and(2 * c + lax.rem(q, 2) == x, c == k)

    def total(q):
        for k in range(2):
            arrived(part_in.at[q, k], s_part_in.at[q, k])
            both = (part[q, k, keep] + part_in[q, k]).astype(bf16)
            here = red_here(q, k)

            @pl.when(here)
            def _():
                red_in[x, q // 2] = both

            @pl.when(jnp.logical_not(here))
            def _():
                red_out[q, k] = both
                red_copy(q, k).start()

        for zz in range(2):
            d, up, down = reach(q, zz)
            for way, on in enumerate((up, down)):
                @pl.when(jnp.logical_or(d == 0, on))
                def _():
                    chain_copy(q, zz, way).wait_send()
                    for k in range(NY):
                        spread_copy(q, zz, k, way).wait_send()
            for k in range(3):
                ring_copy(q, zz, k).wait_send()

        @pl.when(is_root)
        def _():
            for k in range(3):
                edge_copy(q, k).wait_send()

        for k in range(2):
            part_copy(q, k).wait_send()

    first = (hops(1) < hops(0)).astype(jnp.int32)

    def once(t, when, f, *args):
        @pl.when(t == when)
        def _():
            f(*args)

    def normalize_given():
        give.wait_recv()
        normalize(1 - h)

    def normalize_mine():
        for k in range(1, 8):
            slot = lax.rem(2 * own + h + k, 8)
            arrived(squares_in.at[slot], s_sq_in.at[slot])
        normalize(h)

    def turn(t, _):
        once(t, HOP * jnp.minimum(hops(0), hops(1)) + GIVE_T, give.start)
        for i in range(1, 7):
            once(t, i * RELAY_T, pass_word, i)
        for zz in (first, 1 - first):
            flow(t - HOP * hops(zz), zz)
        for zz in range(2):
            each_chunk(t - HOP * hops(zz) - RING_ON, functools.partial(ring_on, zz))
        for zz in range(2):
            each_chunk(t - HOP * hops(zz) - RING_END, functools.partial(ring_end, zz))
        once(t, NORM_T, normalize_mine)
        once(t, LAST - 1, normalize_given)
        each_chunk(t - LAST, dot)
        each_chunk(t - LAST - JOIN, total)
        return 0

    lax.fori_loop(0, STREAM - 4 + LAST + JOIN, turn, 0)

    for k in range(NX):
        @pl.when(jnp.logical_or(x != k, h != c))
        def _():
            for kind in range(2):
                arrived(red_in.at[k, kind], s_red_in.at[k, kind])

    def joined(kind):
        both = red_in[0, kind].astype(f32)
        for k in range(1, NX):
            both = both + red_in[k, kind].astype(f32)
        return both

    gate = joined(0)
    hid[...] = (gate / (1.0 + jnp.exp(-gate)) * joined(1)).astype(bf16)

    for half in range(2):
        wide[...] = hid[:, half * 128 : (half + 1) * 128].astype(f32)
        for k in range(PAIR):
            a2a_out[pl.ds(half * PAIR + k, N_REQ, stride=8), :] = wide[k * N_REQ : (k + 1) * N_REQ, :]

    my_tile = pl.ds(pl.multiple_of(req * 8, 8), 8)

    def send_tile(i, _):
        to_req = lax.rem(req + i, N_REQ)
        src = a2a_out.at[pl.ds(pl.multiple_of(to_req * 8, 8), 8)]
        remote(src, a2a_in.at[my_tile], s_a2a_out, s_a2a_in, (to_req, own)).start()
        return 0

    lax.fori_loop(1, N_REQ, send_tile, 0)
    local_out[...] = lax.dot_general(
        pick[...], hid[...], (((0,), (0,)), ((), ())), preferred_element_type=f32
    ).astype(bf16)
    keep_local = pltpu.make_async_copy(local_out, local_hbm, s_local)
    keep_local.start()
    a2a_in[my_tile, :] = a2a_out[my_tile, :]

    for q in range(NQ):
        for k in range(2):
            @pl.when(jnp.logical_not(red_here(q, k)))
            def _():
                red_copy(q, k).wait_send()
    give.wait_send()
    for cp in sq_sends:
        cp.wait_send()

    @pl.when(jnp.logical_not(self_root))
    def _():
        remote(gate_w, gate_at(own), s_root_out.at[0], s_gate_in.at[own], root).wait_send()
        remote(up_w, root_up.at[own], s_root_out.at[1], s_up_in.at[own], root).wait_send()

    others = pl.ds(0, 8 * (N_REQ - 1))
    arrived(a2a_out.at[others], s_a2a_out)
    arrived(a2a_in.at[others], s_a2a_in)
    for half in range(2):
        for k in range(PAIR):
            wide[pl.ds(k, N_REQ, stride=PAIR), :] = a2a_in[pl.ds(half * PAIR + k, N_REQ, stride=8), :]
        packed_out[:, half * 128 : (half + 1) * 128] = wide[...].astype(bf16)
    keep_local.wait()


def body(tokens, gain, gate_weight, up_weight, lengths, dest, owner):
    vmem = pl.BlockSpec(memory_space=pltpu.VMEM)
    smem = pl.BlockSpec(memory_space=pltpu.SMEM)
    dma = pltpu.SemaphoreType.DMA
    return pl.pallas_call(
        kernel,
        out_shape=(jax.ShapeDtypeStruct((ROWS, HID), bf16), jax.ShapeDtypeStruct((TOK, HID), bf16)),
        in_specs=[vmem, smem, smem, vmem, pl.BlockSpec(memory_space=pl.ANY), vmem, vmem],
        out_specs=(vmem, pl.BlockSpec(memory_space=pl.ANY)),
        scratch_shapes=[
            pltpu.VMEM((TOK, FEAT), bf16),
            pltpu.VMEM((ROWS, TOK), bf16),
            pltpu.VMEM((2 * ROWS, FEAT // 2), bf16),
            pltpu.VMEM((ROWS, FEAT // 2), bf16),
            pltpu.VMEM((NQ, 2, NY, ROWS, WC), bf16),
            pltpu.VMEM((N_OWN, ROWS, HID), bf16),
            pltpu.VMEM((ROWS, 128), f32),
            pltpu.VMEM((8, ROWS), f32),
            pltpu.VMEM((8, 8, ROWS), f32),
            pltpu.VMEM((NQ, 2, 2 * ROWS, HID), f32),
            pltpu.VMEM((NQ, 2, ROWS, HID), f32),
            pltpu.VMEM((NQ, 2, ROWS, HID), bf16),
            pltpu.VMEM((NX, 2, ROWS, HID), bf16),
            pltpu.VMEM((ROWS, HID), bf16),
            pltpu.VMEM((TOK, HID), bf16),
            pltpu.VMEM((8 * N_REQ, 128), f32),
            pltpu.VMEM((8 * N_REQ, 128), f32),
            pltpu.VMEM((ROWS, 128), f32),
            dma, dma((2,)), dma((2,)), dma((N_OWN,)), dma((N_OWN,)), dma((7,)), dma((8,)),
            dma((NQ, 2, 2)), dma((NQ, 2)), dma((NQ, 2, 3)), dma((NQ, 2, 3)), dma((NQ, 3)), dma((NQ, 3)),
            dma((NQ, 2, NY, 2)), dma((NQ, 2, NY)),
            dma((NQ, 2)), dma((NQ, 2)), dma((NQ, 2)), dma((NX, 2)), dma, dma, dma,
            pltpu.SemaphoreType.REGULAR((6,)),
        ],
        compiler_params=pltpu.CompilerParams(
            collective_id=0, has_side_effects=True, vmem_limit_bytes=56 * 2**20
        ),
        name="swiglu_panel",
    )(gain.reshape(1, D), owner, lengths, dest.reshape(1, TOK), tokens, gate_weight, up_weight)


def solution(mesh):
    placed = (P("req", "own"), P(), P("req", "own"), P("req", "own"), P("req"), P("req"), P())
    return jax.shard_map(
        body,
        mesh=mesh,
        in_specs=placed,
        out_specs=(P("req", "own"), P("req", "own")),
        check_vma=False,
    )
```

```python
import functools

import jax
import jax.numpy as jnp
from jax import lax
from jax.experimental import pallas as pl
from jax.experimental.pallas import tpu as pltpu
from jax.sharding import PartitionSpec as P

MESH = pl.DeviceIdType.MESH
f32 = jnp.float32
bf16 = jnp.bfloat16

norm_eps = 1e-05
D = 16384
N_REQ = 64
N_OWN = 4
NX, NY, NZ = 4, 4, 8
TOK = 512
ROWS = 256
HID = 256
FEAT = 4096
PAIR = 4
NQ = 4
WC = 2 * HID
CUT = 160
CHAIN_T = (1, 3, 9, 11)
EDGE_T = (0, 4, 5, 9)
ORDER = (0, 3, 1, 2)
LAGS = (0, 4, 6, 10, 11)
RING_ON, RING_END, JOIN, GIVE_T, RELAY_T = 4, 8, 2, 8, 2
STREAM = 5 * NQ
LOAD_T = tuple(min(a, b) for a, b in zip(CHAIN_T, EDGE_T))
REST_T = [n for n in range(STREAM) if n not in CHAIN_T]
DOT_WAIT = (0, 0, 0, 0)
DOT_T = tuple(LAGS[4] + max(REST_T[4 * q + 3], CHAIN_T[q] + RING_END) + DOT_WAIT[q] for q in range(NQ))
TOTAL_T = [DOT_T[1] + 1]
for done in DOT_T[2:]:
    TOTAL_T.append(max(TOTAL_T[-1] + 1, done))
TOTAL_T.append(TOTAL_T[-1] + 1)


def kernel(
    gain, owner, lengths, dest, tok_hbm, gate_w, up_w,
    packed_out, local_hbm,
    tok, pick, act, act_out, panel, root_up, squares, squares_out, squares_in,
    part, part_in, red_out, red_in, hid, local_out, a2a_out, a2a_in, wide,
    s_tok, s_act, s_root_out, s_gate_in, s_up_in, s_sq_out, s_sq_in,
    s_chain_out, s_chain_in, s_ring_out, s_ring_in, s_edge_out, s_edge_in, s_spread_out, s_spread_in,
    s_part_out, s_part_in, s_red_out, s_red_in, s_a2a_out, s_a2a_in, s_local, relay,
):
    req = lax.axis_index("req")
    own = lax.axis_index("own")
    h, z, y = req // 32, (req // 4) % 8, req % 4
    j, c = own // 2, own % 2
    x = 2 * h + j

    def at(x_, y_, z_, c_):
        x_, y_, z_ = lax.rem(x_ + NX, NX), lax.rem(y_ + NY, NY), lax.rem(z_ + NZ, NZ)
        return ((x_ // 2 * NZ + z_) * NY + y_, (x_ % 2) * 2 + c_)

    def remote(src, dst, send, recv, device):
        return pltpu.make_async_remote_copy(
            src_ref=src, dst_ref=dst, send_sem=send, recv_sem=recv, device_id=device, device_id_type=MESH
        )

    def arrived(ref, sem):
        pltpu.make_async_copy(ref, ref, sem).wait()


    barrier = pltpu.get_barrier_semaphore()
    other_req = lax.rem(req + 32, N_REQ)
    beside = [at(x, y + 1, z, c), at(x, y - 1, z, c)], [at(x, y, z + 1, c), at(x, y, z - 1, c)]
    line = [(req, lax.rem(own + k, N_OWN)) for k in range(1, N_OWN)]
    line += [(other_req, lax.rem(own + k, N_OWN)) for k in range(N_OWN)]
    for device in line + beside[0] + beside[1]:
        pl.semaphore_signal(barrier, inc=1, device_id=device, device_id_type=MESH)

    fetch = pltpu.make_async_copy(tok_hbm, tok, s_tok)
    fetch.start()
    pl.semaphore_wait(barrier, 11)

    def pass_word(i):
        if i > 0:
            pl.semaphore_wait(relay.at[i - 1], 2)
        if i < 6:
            for device in beside[0 if i < 2 else 1]:
                pl.semaphore_signal(relay.at[i], inc=1, device_id=device, device_id_type=MESH)

    root = at(2 * (z % 2) + h, y, z, z // 4)
    self_root = jnp.logical_and(2 * (z % 2) + h == x, z // 4 == c)
    is_root = jnp.logical_and(z % 2 == h, z // 4 == c)
    zr = (z % 4) // 2

    def gate_at(k):
        return panel.at[k // 2, zr, y, :, pl.ds(pl.multiple_of(k % 2 * HID, HID), HID)]

    def to_root(src, dst, out, into):
        @pl.when(self_root)
        def _():
            pltpu.make_async_copy(src, dst, into).start()

        @pl.when(jnp.logical_not(self_root))
        def _():
            remote(src, dst, out, into, root).start()

    def gates_to_root():
        to_root(gate_w, gate_at(own), s_root_out.at[0], s_gate_in.at[own])

    def ups_to_root():
        to_root(up_w, root_up.at[own], s_root_out.at[1], s_up_in.at[own])

    gates_to_root()

    pass_word(0)

    slot = lax.broadcasted_iota(jnp.int32, (1, TOK), 1)
    span = jnp.where(
        slot < 128, lengths[0], jnp.where(slot < 256, lengths[1], jnp.where(slot < 384, lengths[2], lengths[3]))
    )
    live = (slot % 128) < span
    to = jnp.where(live, dest[...], -1)
    marks = (lax.broadcasted_iota(jnp.int32, (N_REQ, TOK), 0) == to).astype(f32)
    earlier = lax.broadcasted_iota(jnp.int32, (TOK, TOK), 0) < lax.broadcasted_iota(jnp.int32, (TOK, TOK), 1)
    before = jnp.dot(marks.astype(bf16), earlier.astype(f32).astype(bf16), preferred_element_type=f32)
    rank = jnp.sum(before * marks, axis=0, keepdims=True)
    row = jnp.where(live, rank * N_REQ + to.astype(f32), -1.0)
    pick[...] = (lax.broadcasted_iota(jnp.int32, (ROWS, TOK), 0).astype(f32) == row).astype(f32).astype(bf16)
    fetch.wait()

    mine = pl.ds(pl.multiple_of(h * ROWS, ROWS), ROWS)

    def arrange(block, out):
        col = pl.multiple_of(block * 1024, 1024)
        rows = jnp.dot(pick[...], tok[:, pl.ds(col, 1024)], preferred_element_type=f32)
        sq = rows * rows
        for k in range(8):
            squares[...] += sq[:, k * 128 : (k + 1) * 128]
        out[...] = rows.astype(bf16)

    squares[...] = jnp.zeros_like(squares)
    for zz in range(2):
        arrange(1 - h + 2 * zz, act_out.at[:, pl.ds(zz * 1024, 1024)])
    for zz in range(2):
        arrange(h + 2 * zz, act.at[mine, pl.ds(zz * 1024, 1024)])

    partner = (other_req, own)
    give = remote(act_out, act.at[mine], s_act.at[0], s_act.at[1], partner)

    def turned(a, axis):
        eye = lax.broadcasted_iota(jnp.int32, (ROWS, ROWS), 0) == lax.broadcasted_iota(jnp.int32, (ROWS, ROWS), 1)
        return jnp.sum(jnp.where(eye, a, 0.0), axis=axis, keepdims=True)

    row_sums = turned(jnp.sum(squares[...], axis=1, keepdims=True), 0)
    squares_out[...] = jnp.broadcast_to(row_sums, (8, ROWS))
    sq_sends = []
    for k, device in enumerate(line):
        cp = remote(squares_out, squares_in.at[2 * own + h], s_sq_out.at[k], s_sq_in.at[2 * own + h], device)
        cp.start()
        sq_sends.append(cp)
    squares_in[2 * own + h] = squares_out[...]

    def normalize(hh):
        sums = squares_in[hh, 0:1, :]
        for k in range(1, N_OWN):
            sums = sums + squares_in[2 * k + hh, 0:1, :]
        scale = lax.rsqrt(turned(sums, 1) * (1.0 / D) + norm_eps)
        rows = pl.ds(pl.multiple_of(hh * ROWS, ROWS), ROWS)
        for zz in range(2):
            for n in range(2):
                cols = pl.ds(zz * 1024 + n * 512, 512)
                here = pl.multiple_of(own * FEAT + (h + 2 * zz) * 1024 + n * 512, 512)
                act[rows, cols] = (act[rows, cols].astype(f32) * scale * gain[:, pl.ds(here, 512)]).astype(bf16)

    def block(q, zz, yy, rows):
        return panel.at[q, zz, yy, pl.ds(rows[0], rows[1])]

    ra, rb = (0, CUT), (CUT, ROWS - CUT)

    def z_next(way):
        return at(x, y, z + 1 - 2 * way, c)

    def chain_copy(q, zz, way):
        ref = block(q, zz, y, ra)
        return remote(ref, ref, s_chain_out.at[q, zz, way], s_chain_in.at[q, zz], z_next(way))

    def spread_copy(q, zz, k, way):
        ref = block(q, zz, lax.rem(y + k, NY), rb)
        return remote(ref, ref, s_spread_out.at[q, zz, k, way], s_spread_in.at[q, zz, k], z_next(way))

    def y_copy(q, zz, k, rows, out, into, turn):
        way = turn if k == 2 else k
        yy = lax.rem(y + 3 - 2 * way, NY) if k == 2 else y
        ref = block(q, zz, yy, rows)
        return remote(ref, ref, out, into, at(x, y + 1 - 2 * way, z, c))

    def ring_copy(q, zz, k):
        return y_copy(q, zz, k, ra, s_ring_out.at[q, zz, k], s_ring_in.at[q, zz, k], zz)

    def edge_copy(q, k):
        return y_copy(q, zr, k, rb, s_edge_out.at[q, k], s_edge_in.at[q, k], lax.rem(q, 2))

    def y_arrived(q, zz, k, rows, into, turn):
        step = 2 if k == 2 else 3 - 2 * k
        arrived(block(q, zz, lax.rem(y + step, NY), rows), into)

    def reach(q, zz):
        d = lax.rem(z - (4 * c + h + 2 * zz) + 2 * NZ, NZ)
        far = 4 - lax.rem(q + zz, 2)
        return d, jnp.logical_and(d > 0, d < far), d >= far + 2

    def hops(zz):
        d = lax.rem(z - (4 * c + h + 2 * zz) + 2 * NZ, NZ)
        return jnp.minimum(d, NZ - d)

    def load_panel(q):
        @pl.when(q < 2)
        def _():
            for k in range(2):
                arrived(gate_at(2 * q + k), s_gate_in.at[2 * q + k])

        @pl.when(q == 2)
        def _():
            for k in range(N_OWN):
                arrived(root_up.at[k], s_up_in.at[k])

        @pl.when(q >= 2)
        def _():
            for k in range(2):
                stored = jnp.int32(0)
                for m in range(1, N_OWN):
                    stored = jnp.where(owner[m] == 2 * (q - 2) + k, m, stored)
                panel[q, zr, y, :, k * HID : (k + 1) * HID] = root_up[stored]

    def open_edges(q):
        for k in range(2):
            edge_copy(q, k).start()

    def on_chain(q, zz):
        d, up, down = reach(q, zz)

        @pl.when(d == 0)
        def _():
            for way in range(2):
                chain_copy(q, zz, way).start()

        @pl.when(d > 0)
        def _():
            arrived(block(q, zz, y, ra), s_chain_in.at[q, zz])

            @pl.when(jnp.logical_or(up, down))
            def _():
                chain_copy(q, zz, down.astype(jnp.int32)).start()

        for k in range(2):
            ring_copy(q, zz, k).start()

    def on_spread(q, zz, i):
        k = pick_from(ORDER, i)
        d, up, down = reach(q, zz)

        @pl.when(d == 0)
        def _():
            @pl.when(k > 0)
            def _():
                e = jnp.where(k == 3, 0, k)
                arrived(block(q, zz, lax.rem(y + k, NY), rb), s_edge_in.at[q, e])

                @pl.when(e == lax.rem(q, 2))
                def _():
                    edge_copy(q, 2).start()

            for way in range(2):
                spread_copy(q, zz, k, way).start()

        @pl.when(d > 0)
        def _():
            arrived(block(q, zz, lax.rem(y + k, NY), rb), s_spread_in.at[q, zz, k])

            @pl.when(jnp.logical_or(up, down))
            def _():
                spread_copy(q, zz, k, down.astype(jnp.int32)).start()

    def pick_from(table, i):
        out = jnp.int32(table[0])
        for k in range(1, len(table)):
            out = jnp.where(i >= k, table[k], out)
        return out

    def which(n, table):
        n_before, hit = jnp.int32(0), n == table[0]
        for v in table:
            n_before = n_before + (n > v).astype(jnp.int32)
            hit = jnp.logical_or(hit, n == v)
        return n_before, hit

    def flow(n, zz):
        @pl.when(jnp.logical_and(n >= 0, n < STREAM))
        def _():
            @pl.when(jnp.logical_and(is_root, zr == zz))
            def _():
                for table, f in ((LOAD_T, load_panel), (EDGE_T, open_edges)):
                    q, hit = which(n, table)

                    @pl.when(hit)
                    def _():
                        f(q)

            q, hit = which(n, CHAIN_T)

            @pl.when(hit)
            def _():
                on_chain(q, zz)

            @pl.when(jnp.logical_not(hit))
            def _():
                on_spread((n - q) // 4, zz, lax.rem(n - q, 4))

    def each_chunk(n, table, f):
        q, hit = which(n, table)

        @pl.when(hit)
        def _():
            f(q)

    def ring_on(zz, q):
        y_arrived(q, zz, zz, ra, s_ring_in.at[q, zz, zz], zz)
        ring_copy(q, zz, 2).start()

    def ring_end(zz, q):
        y_arrived(q, zz, 1 - zz, ra, s_ring_in.at[q, zz, 1 - zz], zz)
        y_arrived(q, zz, 2, ra, s_ring_in.at[q, zz, 2], zz)

    keep = pl.ds(pl.multiple_of(c * ROWS, ROWS), ROWS)
    pass_on = pl.ds(pl.multiple_of((1 - c) * ROWS, ROWS), ROWS)

    def part_copy(q, k):
        return remote(
            part.at[q, k, pass_on], part_in.at[q, k], s_part_out.at[q, k], s_part_in.at[q, k], (req, 2 * j + 1 - c)
        )

    def dot(q):
        for k in range(2):
            w = panel[q, :, :, :, k * HID : (k + 1) * HID].reshape(8 * ROWS, HID)
            part[q, k] = jnp.dot(act[...], w, preferred_element_type=f32)
            part_copy(q, k).start()

    def red_copy(q, k):
        device = at(2 * c + lax.rem(q, 2), y, z, k)
        return remote(red_out.at[q, k], red_in.at[x, q // 2], s_red_out.at[q, k], s_red_in.at[x, q // 2], device)

    def red_here(q, k):
        return jnp.logical_and(2 * c + lax.rem(q, 2) == x, c == k)

    def total(q):
        for k in range(2):
            arrived(part_in.at[q, k], s_part_in.at[q, k])
            both = (part[q, k, keep] + part_in[q, k]).astype(bf16)
            here = red_here(q, k)

            @pl.when(here)
            def _():
                red_in[x, q // 2] = both

            @pl.when(jnp.logical_not(here))
            def _():
                red_out[q, k] = both
                red_copy(q, k).start()

        for zz in range(2):
            d, up, down = reach(q, zz)
            for way, on in enumerate((up, down)):
                @pl.when(jnp.logical_or(d == 0, on))
                def _():
                    chain_copy(q, zz, way).wait_send()
                    for k in range(NY):
                        spread_copy(q, zz, k, way).wait_send()
            for k in range(3):
                ring_copy(q, zz, k).wait_send()

        @pl.when(is_root)
        def _():
            for k in range(3):
                edge_copy(q, k).wait_send()

        for k in range(2):
            part_copy(q, k).wait_send()

    first = (hops(1) < hops(0)).astype(jnp.int32)

    def once(t, when, f, *args):
        @pl.when(t == when)
        def _():
            f(*args)

    def normalize_given():
        give.wait_recv()
        normalize(1 - h)

    def normalize_mine():
        for k in range(1, 8):
            slot = lax.rem(2 * own + h + k, 8)
            arrived(squares_in.at[slot], s_sq_in.at[slot])
        normalize(h)

    behind = [pick_from(LAGS, hops(zz)) for zz in range(2)]
    near = jnp.minimum(behind[0], behind[1])

    ups_to_root()

    def turn(t, _):
        once(t, near + GIVE_T, give.start)
        for i in range(1, 7):
            once(t, i * RELAY_T, pass_word, i)

        for zz in (first, 1 - first):
            flow(t - jnp.where(zz == 0, behind[0], behind[1]), zz)
        for zz in range(2):
            each_chunk(t - behind[zz] - RING_ON, CHAIN_T, functools.partial(ring_on, zz))
        for zz in range(2):
            each_chunk(t - behind[zz] - RING_END, CHAIN_T, functools.partial(ring_end, zz))

        @pl.when(t == DOT_T[0] - 1)
        def _():
            normalize_mine()
            normalize_given()

        each_chunk(t, DOT_T, dot)
        each_chunk(t, TOTAL_T, total)
        return 0

    lax.fori_loop(0, TOTAL_T[-1] + 1, turn, 0)

    for k in range(NX):
        @pl.when(jnp.logical_or(x != k, h != c))
        def _():
            for kind in range(2):
                arrived(red_in.at[k, kind], s_red_in.at[k, kind])

    def joined(kind):
        both = red_in[0, kind].astype(f32)
        for k in range(1, NX):
            both = both + red_in[k, kind].astype(f32)
        return both

    gate = joined(0)
    hid[...] = (gate / (1.0 + jnp.exp(-gate)) * joined(1)).astype(bf16)

    for half in range(2):
        wide[...] = hid[:, half * 128 : (half + 1) * 128].astype(f32)
        for k in range(PAIR):
            a2a_out[pl.ds(half * PAIR + k, N_REQ, stride=8), :] = wide[k * N_REQ : (k + 1) * N_REQ, :]

    my_tile = pl.ds(pl.multiple_of(req * 8, 8), 8)

    def send_tile(i, _):
        to_req = lax.rem(req + i, N_REQ)
        src = a2a_out.at[pl.ds(pl.multiple_of(to_req * 8, 8), 8)]
        remote(src, a2a_in.at[my_tile], s_a2a_out, s_a2a_in, (to_req, own)).start()
        return 0

    lax.fori_loop(1, N_REQ, send_tile, 0)
    local_out[...] = lax.dot_general(
        pick[...], hid[...], (((0,), (0,)), ((), ())), preferred_element_type=f32
    ).astype(bf16)
    keep_local = pltpu.make_async_copy(local_out, local_hbm, s_local)
    keep_local.start()
    a2a_in[my_tile, :] = a2a_out[my_tile, :]

    for q in range(NQ):
        for k in range(2):
            @pl.when(jnp.logical_not(red_here(q, k)))
            def _():
                red_copy(q, k).wait_send()
    give.wait_send()
    for cp in sq_sends:
        cp.wait_send()

    @pl.when(jnp.logical_not(self_root))
    def _():
        remote(gate_w, gate_at(own), s_root_out.at[0], s_gate_in.at[own], root).wait_send()
        remote(up_w, root_up.at[own], s_root_out.at[1], s_up_in.at[own], root).wait_send()

    others = pl.ds(0, 8 * (N_REQ - 1))
    arrived(a2a_out.at[others], s_a2a_out)
    arrived(a2a_in.at[others], s_a2a_in)
    for half in range(2):
        for k in range(PAIR):
            wide[pl.ds(k, N_REQ, stride=PAIR), :] = a2a_in[pl.ds(half * PAIR + k, N_REQ, stride=8), :]
        packed_out[:, half * 128 : (half + 1) * 128] = wide[...].astype(bf16)
    keep_local.wait()


def body(tokens, gain, gate_weight, up_weight, lengths, dest, owner):
    vmem = pl.BlockSpec(memory_space=pltpu.VMEM)
    smem = pl.BlockSpec(memory_space=pltpu.SMEM)
    dma = pltpu.SemaphoreType.DMA
    return pl.pallas_call(
        kernel,
        out_shape=(jax.ShapeDtypeStruct((ROWS, HID), bf16), jax.ShapeDtypeStruct((TOK, HID), bf16)),
        in_specs=[vmem, smem, smem, vmem, pl.BlockSpec(memory_space=pl.ANY), vmem, vmem],
        out_specs=(vmem, pl.BlockSpec(memory_space=pl.ANY)),
        scratch_shapes=[
            pltpu.VMEM((TOK, FEAT), bf16),
            pltpu.VMEM((ROWS, TOK), bf16),
            pltpu.VMEM((2 * ROWS, FEAT // 2), bf16),
            pltpu.VMEM((ROWS, FEAT // 2), bf16),
            pltpu.VMEM((NQ, 2, NY, ROWS, WC), bf16),
            pltpu.VMEM((N_OWN, ROWS, HID), bf16),
            pltpu.VMEM((ROWS, 128), f32),
            pltpu.VMEM((8, ROWS), f32),
            pltpu.VMEM((8, 8, ROWS), f32),
            pltpu.VMEM((NQ, 2, 2 * ROWS, HID), f32),
            pltpu.VMEM((NQ, 2, ROWS, HID), f32),
            pltpu.VMEM((NQ, 2, ROWS, HID), bf16),
            pltpu.VMEM((NX, 2, ROWS, HID), bf16),
            pltpu.VMEM((ROWS, HID), bf16),
            pltpu.VMEM((TOK, HID), bf16),
            pltpu.VMEM((8 * N_REQ, 128), f32),
            pltpu.VMEM((8 * N_REQ, 128), f32),
            pltpu.VMEM((ROWS, 128), f32),
            dma, dma((2,)), dma((2,)), dma((N_OWN,)), dma((N_OWN,)), dma((7,)), dma((8,)),
            dma((NQ, 2, 2)), dma((NQ, 2)), dma((NQ, 2, 3)), dma((NQ, 2, 3)), dma((NQ, 3)), dma((NQ, 3)),
            dma((NQ, 2, NY, 2)), dma((NQ, 2, NY)),
            dma((NQ, 2)), dma((NQ, 2)), dma((NQ, 2)), dma((NX, 2)), dma, dma, dma,
            pltpu.SemaphoreType.REGULAR((6,)),
        ],
        compiler_params=pltpu.CompilerParams(
            collective_id=0, has_side_effects=True, vmem_limit_bytes=56 * 2**20
        ),
        name="swiglu_panel",
    )(gain.reshape(1, D), owner, lengths, dest.reshape(1, TOK), tokens, gate_weight, up_weight)


def solution(mesh):
    placed = (P("req", "own"), P(), P("req", "own"), P("req", "own"), P("req"), P("req"), P())
    return jax.shard_map(
        body,
        mesh=mesh,
        in_specs=placed,
        out_specs=(P("req", "own"), P("req", "own")),
        check_vma=False,
    )
```

```python
import functools

import jax
import jax.numpy as jnp
from jax import lax
from jax.experimental import pallas as pl
from jax.experimental.pallas import tpu as pltpu
from jax.sharding import PartitionSpec as P

MESH = pl.DeviceIdType.MESH
f32 = jnp.float32
bf16 = jnp.bfloat16

norm_eps = 1e-05
D = 16384
N_REQ = 64
N_OWN = 4
NX, NY, NZ = 4, 4, 8
TOK = 512
ROWS = 256
HID = 256
GROUPS = 2
PART = ROWS // GROUPS
PEERS = N_REQ // GROUPS
FEAT = 4096
PAIR = 4
NQ = 4
WC = 2 * HID
CUT = 160
CHAIN_T = (1, 3, 9, 11)
EDGE_T = (0, 4, 5, 9)
ORDER = (0, 3, 1, 2)
LAGS = (0, 4, 6, 10, 11)
RING_ON, RING_END, JOIN, GIVE_T, RELAY_T = 4, 8, 2, 8, 2
STREAM = 5 * NQ
LOAD_T = tuple(min(a, b) for a, b in zip(CHAIN_T, EDGE_T))
REST_T = [n for n in range(STREAM) if n not in CHAIN_T]
DOT_WAIT = (0, 0, 0, 0)
DOT_T = tuple(LAGS[4] + max(REST_T[4 * q + 3], CHAIN_T[q] + RING_END) + DOT_WAIT[q] for q in range(NQ))
TOTAL_T = [DOT_T[1] + 1]
for done in DOT_T[2:]:
    TOTAL_T.append(max(TOTAL_T[-1] + 1, done))
TOTAL_T.append(TOTAL_T[-1] + 1)


def kernel(
    gain, owner, lengths, dest, tok_hbm, gate_w, up_w,
    packed_out, local_hbm,
    tok, pick, act, act_out, panel, root_up, squares, squares_out, squares_in,
    part, part_in, red_out, red_in, hid, local_out, a2a_out, a2a_in, wide,
    s_tok, s_act, s_root_out, s_gate_in, s_up_in, s_sq_out, s_sq_in,
    s_chain_out, s_chain_in, s_ring_out, s_ring_in, s_edge_out, s_edge_in, s_spread_out, s_spread_in,
    s_part_out, s_part_in, s_red_out, s_red_in, s_a2a_out, s_a2a_in, s_local, relay,
):
    req = lax.axis_index("req")
    own = lax.axis_index("own")
    h, z, y = req // 32, (req // 4) % 8, req % 4
    j, c = own // 2, own % 2
    x = 2 * h + j

    def at(x_, y_, z_, c_):
        x_, y_, z_ = lax.rem(x_ + NX, NX), lax.rem(y_ + NY, NY), lax.rem(z_ + NZ, NZ)
        return ((x_ // 2 * NZ + z_) * NY + y_, (x_ % 2) * 2 + c_)

    def remote(src, dst, send, recv, device):
        return pltpu.make_async_remote_copy(
            src_ref=src, dst_ref=dst, send_sem=send, recv_sem=recv, device_id=device, device_id_type=MESH
        )

    def arrived(ref, sem):
        pltpu.make_async_copy(ref, ref, sem).wait()


    barrier = pltpu.get_barrier_semaphore()
    other_req = lax.rem(req + 32, N_REQ)
    beside = [at(x, y + 1, z, c), at(x, y - 1, z, c)], [at(x, y, z + 1, c), at(x, y, z - 1, c)]
    line = [(req, lax.rem(own + k, N_OWN)) for k in range(1, N_OWN)]
    line += [(other_req, lax.rem(own + k, N_OWN)) for k in range(N_OWN)]
    for device in line + beside[0] + beside[1]:
        pl.semaphore_signal(barrier, inc=1, device_id=device, device_id_type=MESH)

    fetch = pltpu.make_async_copy(tok_hbm, tok, s_tok)
    fetch.start()
    pl.semaphore_wait(barrier, 11)

    def pass_word(i):
        if i > 0:
            pl.semaphore_wait(relay.at[i - 1], 2)
        if i < 6:
            for device in beside[0 if i < 2 else 1]:
                pl.semaphore_signal(relay.at[i], inc=1, device_id=device, device_id_type=MESH)

    root = at(2 * (z % 2) + h, y, z, z // 4)
    self_root = jnp.logical_and(2 * (z % 2) + h == x, z // 4 == c)
    is_root = jnp.logical_and(z % 2 == h, z // 4 == c)
    zr = (z % 4) // 2

    def gate_at(k):
        return panel.at[k // 2, zr, y, :, pl.ds(pl.multiple_of(k % 2 * HID, HID), HID)]

    def to_root(src, dst, out, into):
        @pl.when(self_root)
        def _():
            pltpu.make_async_copy(src, dst, into).start()

        @pl.when(jnp.logical_not(self_root))
        def _():
            remote(src, dst, out, into, root).start()

    def gates_to_root():
        to_root(gate_w, gate_at(own), s_root_out.at[0], s_gate_in.at[own])

    def ups_to_root():
        to_root(up_w, root_up.at[own], s_root_out.at[1], s_up_in.at[own])

    gates_to_root()

    pass_word(0)

    slot = lax.broadcasted_iota(jnp.int32, (1, TOK), 1)
    span = jnp.where(
        slot < 128, lengths[0], jnp.where(slot < 256, lengths[1], jnp.where(slot < 384, lengths[2], lengths[3]))
    )
    live = (slot % 128) < span
    to = jnp.where(live, dest[...], -1)
    marks = (lax.broadcasted_iota(jnp.int32, (N_REQ, TOK), 0) == to).astype(f32)
    earlier = lax.broadcasted_iota(jnp.int32, (TOK, TOK), 0) < lax.broadcasted_iota(jnp.int32, (TOK, TOK), 1)
    before = jnp.dot(marks.astype(bf16), earlier.astype(f32).astype(bf16), preferred_element_type=f32)
    rank = jnp.sum(before * marks, axis=0, keepdims=True)
    row = jnp.where(live, rank * PEERS + (to // PEERS * PART + to % PEERS).astype(f32), -1.0)
    pick[...] = (lax.broadcasted_iota(jnp.int32, (ROWS, TOK), 0).astype(f32) == row).astype(f32).astype(bf16)
    fetch.wait()

    mine = pl.ds(pl.multiple_of(h * ROWS, ROWS), ROWS)

    def arrange(block, out):
        col = pl.multiple_of(block * 1024, 1024)
        rows = jnp.dot(pick[...], tok[:, pl.ds(col, 1024)], preferred_element_type=f32)
        sq = rows * rows
        for k in range(8):
            squares[...] += sq[:, k * 128 : (k + 1) * 128]
        out[...] = rows.astype(bf16)

    squares[...] = jnp.zeros_like(squares)
    for zz in range(2):
        arrange(1 - h + 2 * zz, act_out.at[:, pl.ds(zz * 1024, 1024)])
    for zz in range(2):
        arrange(h + 2 * zz, act.at[mine, pl.ds(zz * 1024, 1024)])

    partner = (other_req, own)
    give = remote(act_out, act.at[mine], s_act.at[0], s_act.at[1], partner)

    def turned(a, axis):
        eye = lax.broadcasted_iota(jnp.int32, (ROWS, ROWS), 0) == lax.broadcasted_iota(jnp.int32, (ROWS, ROWS), 1)
        return jnp.sum(jnp.where(eye, a, 0.0), axis=axis, keepdims=True)

    row_sums = turned(jnp.sum(squares[...], axis=1, keepdims=True), 0)
    squares_out[...] = jnp.broadcast_to(row_sums, (8, ROWS))
    sq_sends = []
    for k, device in enumerate(line):
        cp = remote(squares_out, squares_in.at[2 * own + h], s_sq_out.at[k], s_sq_in.at[2 * own + h], device)
        cp.start()
        sq_sends.append(cp)
    squares_in[2 * own + h] = squares_out[...]

    def normalize(hh):
        sums = squares_in[hh, 0:1, :]
        for k in range(1, N_OWN):
            sums = sums + squares_in[2 * k + hh, 0:1, :]
        scale = lax.rsqrt(turned(sums, 1) * (1.0 / D) + norm_eps)
        rows = pl.ds(pl.multiple_of(hh * ROWS, ROWS), ROWS)
        for zz in range(2):
            for n in range(2):
                cols = pl.ds(zz * 1024 + n * 512, 512)
                here = pl.multiple_of(own * FEAT + (h + 2 * zz) * 1024 + n * 512, 512)
                act[rows, cols] = (act[rows, cols].astype(f32) * scale * gain[:, pl.ds(here, 512)]).astype(bf16)

    def block(q, zz, yy, rows):
        return panel.at[q, zz, yy, pl.ds(rows[0], rows[1])]

    ra, rb = (0, CUT), (CUT, ROWS - CUT)

    def z_next(way):
        return at(x, y, z + 1 - 2 * way, c)

    def chain_copy(q, zz, way):
        ref = block(q, zz, y, ra)
        return remote(ref, ref, s_chain_out.at[q, zz, way], s_chain_in.at[q, zz], z_next(way))

    def spread_copy(q, zz, k, way):
        ref = block(q, zz, lax.rem(y + k, NY), rb)
        return remote(ref, ref, s_spread_out.at[q, zz, k, way], s_spread_in.at[q, zz, k], z_next(way))

    def y_copy(q, zz, k, rows, out, into, turn):
        way = turn if k == 2 else k
        yy = lax.rem(y + 3 - 2 * way, NY) if k == 2 else y
        ref = block(q, zz, yy, rows)
        return remote(ref, ref, out, into, at(x, y + 1 - 2 * way, z, c))

    def ring_copy(q, zz, k):
        return y_copy(q, zz, k, ra, s_ring_out.at[q, zz, k], s_ring_in.at[q, zz, k], zz)

    def edge_copy(q, k):
        return y_copy(q, zr, k, rb, s_edge_out.at[q, k], s_edge_in.at[q, k], lax.rem(q, 2))

    def y_arrived(q, zz, k, rows, into, turn):
        step = 2 if k == 2 else 3 - 2 * k
        arrived(block(q, zz, lax.rem(y + step, NY), rows), into)

    def reach(q, zz):
        d = lax.rem(z - (4 * c + h + 2 * zz) + 2 * NZ, NZ)
        far = 4 - lax.rem(q + zz, 2)
        return d, jnp.logical_and(d > 0, d < far), d >= far + 2

    def hops(zz):
        d = lax.rem(z - (4 * c + h + 2 * zz) + 2 * NZ, NZ)
        return jnp.minimum(d, NZ - d)

    def load_panel(q):
        @pl.when(q < 2)
        def _():
            for k in range(2):
                arrived(gate_at(2 * q + k), s_gate_in.at[2 * q + k])

        @pl.when(q == 2)
        def _():
            for k in range(N_OWN):
                arrived(root_up.at[k], s_up_in.at[k])

        @pl.when(q >= 2)
        def _():
            for k in range(2):
                stored = jnp.int32(0)
                for m in range(1, N_OWN):
                    stored = jnp.where(owner[m] == 2 * (q - 2) + k, m, stored)
                panel[q, zr, y, :, k * HID : (k + 1) * HID] = root_up[stored]

    def open_edges(q):
        for k in range(2):
            edge_copy(q, k).start()

    def on_chain(q, zz):
        d, up, down = reach(q, zz)

        @pl.when(d == 0)
        def _():
            for way in range(2):
                chain_copy(q, zz, way).start()

        @pl.when(d > 0)
        def _():
            arrived(block(q, zz, y, ra), s_chain_in.at[q, zz])

            @pl.when(jnp.logical_or(up, down))
            def _():
                chain_copy(q, zz, down.astype(jnp.int32)).start()

        for k in range(2):
            ring_copy(q, zz, k).start()

    def on_spread(q, zz, i):
        k = pick_from(ORDER, i)
        d, up, down = reach(q, zz)

        @pl.when(d == 0)
        def _():
            @pl.when(k > 0)
            def _():
                e = jnp.where(k == 3, 0, k)
                arrived(block(q, zz, lax.rem(y + k, NY), rb), s_edge_in.at[q, e])

                @pl.when(e == lax.rem(q, 2))
                def _():
                    edge_copy(q, 2).start()

            for way in range(2):
                spread_copy(q, zz, k, way).start()

        @pl.when(d > 0)
        def _():
            arrived(block(q, zz, lax.rem(y + k, NY), rb), s_spread_in.at[q, zz, k])

            @pl.when(jnp.logical_or(up, down))
            def _():
                spread_copy(q, zz, k, down.astype(jnp.int32)).start()

    def pick_from(table, i):
        out = jnp.int32(table[0])
        for k in range(1, len(table)):
            out = jnp.where(i >= k, table[k], out)
        return out

    def which(n, table):
        n_before, hit = jnp.int32(0), n == table[0]
        for v in table:
            n_before = n_before + (n > v).astype(jnp.int32)
            hit = jnp.logical_or(hit, n == v)
        return n_before, hit

    def flow(n, zz):
        @pl.when(jnp.logical_and(n >= 0, n < STREAM))
        def _():
            @pl.when(jnp.logical_and(is_root, zr == zz))
            def _():
                for table, f in ((LOAD_T, load_panel), (EDGE_T, open_edges)):
                    q, hit = which(n, table)

                    @pl.when(hit)
                    def _():
                        f(q)

            q, hit = which(n, CHAIN_T)

            @pl.when(hit)
            def _():
                on_chain(q, zz)

            @pl.when(jnp.logical_not(hit))
            def _():
                on_spread((n - q) // 4, zz, lax.rem(n - q, 4))

    def each_chunk(n, table, f):
        q, hit = which(n, table)

        @pl.when(hit)
        def _():
            f(q)

    def ring_on(zz, q):
        y_arrived(q, zz, zz, ra, s_ring_in.at[q, zz, zz], zz)
        ring_copy(q, zz, 2).start()

    def ring_end(zz, q):
        y_arrived(q, zz, 1 - zz, ra, s_ring_in.at[q, zz, 1 - zz], zz)
        y_arrived(q, zz, 2, ra, s_ring_in.at[q, zz, 2], zz)

    def part_copy(q, k, g):
        here, there = pl.ds(pl.multiple_of((1 - c) * ROWS + g * PART, PART), PART), pl.ds(g * PART, PART)
        return remote(
            part.at[q, k, here], part_in.at[q, k, there],
            s_part_out.at[q, k, g], s_part_in.at[q, k, g], (req, 2 * j + 1 - c),
        )

    def dot(q):
        for k in range(2):
            w = panel[q, :, :, :, k * HID : (k + 1) * HID].reshape(8 * ROWS, HID)
            part[q, k] = jnp.dot(act[...], w, preferred_element_type=f32)
            for g in range(GROUPS):
                part_copy(q, k, g).start()

    def red_copy(q, k, g):
        device = at(2 * c + lax.rem(q, 2), y, z, k)
        rows = pl.ds(g * PART, PART)
        return remote(
            red_out.at[q, k, rows], red_in.at[x, q // 2, rows],
            s_red_out.at[q, k, g], s_red_in.at[x, q // 2, g], device,
        )

    def red_here(q, k):
        return jnp.logical_and(2 * c + lax.rem(q, 2) == x, c == k)

    def total(q):
        for g in range(GROUPS):
            rows = pl.ds(g * PART, PART)
            mine_g = pl.ds(pl.multiple_of(c * ROWS + g * PART, PART), PART)
            for k in range(2):
                arrived(part_in.at[q, k, rows], s_part_in.at[q, k, g])
                both = (part[q, k, mine_g] + part_in[q, k, rows]).astype(bf16)
                here = red_here(q, k)

                @pl.when(here)
                def _():
                    red_in[x, q // 2, rows] = both

                @pl.when(jnp.logical_not(here))
                def _():
                    red_out[q, k, rows] = both
                    red_copy(q, k, g).start()

    def left(q):
        for zz in range(2):
            d, up, down = reach(q, zz)
            for way, on in enumerate((up, down)):
                @pl.when(jnp.logical_or(d == 0, on))
                def _():
                    chain_copy(q, zz, way).wait_send()
                    for k in range(NY):
                        spread_copy(q, zz, k, way).wait_send()
            for k in range(3):
                ring_copy(q, zz, k).wait_send()

        @pl.when(is_root)
        def _():
            for k in range(3):
                edge_copy(q, k).wait_send()

        for k in range(2):
            for g in range(GROUPS):
                part_copy(q, k, g).wait_send()

    first = (hops(1) < hops(0)).astype(jnp.int32)

    def once(t, when, f, *args):
        @pl.when(t == when)
        def _():
            f(*args)

    def normalize_given():
        give.wait_recv()
        normalize(1 - h)

    def normalize_mine():
        for k in range(1, 8):
            slot = lax.rem(2 * own + h + k, 8)
            arrived(squares_in.at[slot], s_sq_in.at[slot])
        normalize(h)

    behind = [pick_from(LAGS, hops(zz)) for zz in range(2)]
    near = jnp.minimum(behind[0], behind[1])

    ups_to_root()

    def turn(t, _):
        once(t, near + GIVE_T, give.start)
        for i in range(1, 7):
            once(t, i * RELAY_T, pass_word, i)

        for zz in (first, 1 - first):
            flow(t - jnp.where(zz == 0, behind[0], behind[1]), zz)
        for zz in range(2):
            each_chunk(t - behind[zz] - RING_ON, CHAIN_T, functools.partial(ring_on, zz))
        for zz in range(2):
            each_chunk(t - behind[zz] - RING_END, CHAIN_T, functools.partial(ring_end, zz))

        @pl.when(t == DOT_T[0] - 1)
        def _():
            normalize_mine()
            normalize_given()

        each_chunk(t, DOT_T, dot)
        each_chunk(t, TOTAL_T, total)
        each_chunk(t, TOTAL_T[:-1], left)
        return 0

    lax.fori_loop(0, TOTAL_T[-1] + 1, turn, 0)

    my_tile = pl.ds(pl.multiple_of(req * 8, 8), 8)

    def send_tile(to_req):
        src = a2a_out.at[pl.ds(pl.multiple_of(to_req * 8, 8), 8)]
        remote(src, a2a_in.at[my_tile], s_a2a_out, s_a2a_in, (to_req, own)).start()

    for g in range(GROUPS):
        rows = pl.ds(g * PART, PART)
        for k in range(NX):
            @pl.when(jnp.logical_or(x != k, h != c))
            def _():
                for kind in range(2):
                    arrived(red_in.at[k, kind, rows], s_red_in.at[k, kind, g])

        gate, up = red_in[0, 0, rows].astype(f32), red_in[0, 1, rows].astype(f32)
        for k in range(1, NX):
            gate = gate + red_in[k, 0, rows].astype(f32)
            up = up + red_in[k, 1, rows].astype(f32)
        hidden = (gate / (1.0 + jnp.exp(-gate)) * up).astype(bf16)
        hid[rows] = hidden
        hidden = hidden.astype(f32)
        for half in range(2):
            for k in range(PAIR):
                a2a_out[pl.ds(g * 8 * PEERS + half * PAIR + k, PEERS, stride=8), :] = hidden[
                    k * PEERS : (k + 1) * PEERS, half * 128 : (half + 1) * 128
                ]

        def send_near(i, _):
            send_tile(PEERS * g + lax.rem(req + i, PEERS))
            return 0

        lax.fori_loop(1, PEERS, send_near, 0)

        @pl.when(req // PEERS != g)
        def _():
            send_tile(PEERS * g + lax.rem(req, PEERS))

    local_out[...] = lax.dot_general(
        pick[...], hid[...], (((0,), (0,)), ((), ())), preferred_element_type=f32
    ).astype(bf16)
    keep_local = pltpu.make_async_copy(local_out, local_hbm, s_local)
    keep_local.start()
    a2a_in[my_tile, :] = a2a_out[my_tile, :]

    left(NQ - 1)
    for q in range(NQ):
        for k in range(2):
            @pl.when(jnp.logical_not(red_here(q, k)))
            def _():
                for g in range(GROUPS):
                    red_copy(q, k, g).wait_send()
    give.wait_send()
    for cp in sq_sends:
        cp.wait_send()

    @pl.when(jnp.logical_not(self_root))
    def _():
        remote(gate_w, gate_at(own), s_root_out.at[0], s_gate_in.at[own], root).wait_send()
        remote(up_w, root_up.at[own], s_root_out.at[1], s_up_in.at[own], root).wait_send()

    others = pl.ds(0, 8 * (N_REQ - 1))
    arrived(a2a_out.at[others], s_a2a_out)
    arrived(a2a_in.at[others], s_a2a_in)
    for half in range(2):
        for k in range(PAIR):
            wide[pl.ds(k, N_REQ, stride=PAIR), :] = a2a_in[pl.ds(half * PAIR + k, N_REQ, stride=8), :]
        packed_out[:, half * 128 : (half + 1) * 128] = wide[...].astype(bf16)
    keep_local.wait()


def body(tokens, gain, gate_weight, up_weight, lengths, dest, owner):
    vmem = pl.BlockSpec(memory_space=pltpu.VMEM)
    smem = pl.BlockSpec(memory_space=pltpu.SMEM)
    dma = pltpu.SemaphoreType.DMA
    return pl.pallas_call(
        kernel,
        out_shape=(jax.ShapeDtypeStruct((ROWS, HID), bf16), jax.ShapeDtypeStruct((TOK, HID), bf16)),
        in_specs=[vmem, smem, smem, vmem, pl.BlockSpec(memory_space=pl.ANY), vmem, vmem],
        out_specs=(vmem, pl.BlockSpec(memory_space=pl.ANY)),
        scratch_shapes=[
            pltpu.VMEM((TOK, FEAT), bf16),
            pltpu.VMEM((ROWS, TOK), bf16),
            pltpu.VMEM((2 * ROWS, FEAT // 2), bf16),
            pltpu.VMEM((ROWS, FEAT // 2), bf16),
            pltpu.VMEM((NQ, 2, NY, ROWS, WC), bf16),
            pltpu.VMEM((N_OWN, ROWS, HID), bf16),
            pltpu.VMEM((ROWS, 128), f32),
            pltpu.VMEM((8, ROWS), f32),
            pltpu.VMEM((8, 8, ROWS), f32),
            pltpu.VMEM((NQ, 2, 2 * ROWS, HID), f32),
            pltpu.VMEM((NQ, 2, ROWS, HID), f32),
            pltpu.VMEM((NQ, 2, ROWS, HID), bf16),
            pltpu.VMEM((NX, 2, ROWS, HID), bf16),
            pltpu.VMEM((ROWS, HID), bf16),
            pltpu.VMEM((TOK, HID), bf16),
            pltpu.VMEM((8 * N_REQ, 128), f32),
            pltpu.VMEM((8 * N_REQ, 128), f32),
            pltpu.VMEM((ROWS, 128), f32),
            dma, dma((2,)), dma((2,)), dma((N_OWN,)), dma((N_OWN,)), dma((7,)), dma((8,)),
            dma((NQ, 2, 2)), dma((NQ, 2)), dma((NQ, 2, 3)), dma((NQ, 2, 3)), dma((NQ, 3)), dma((NQ, 3)),
            dma((NQ, 2, NY, 2)), dma((NQ, 2, NY)),
            dma((NQ, 2, GROUPS)), dma((NQ, 2, GROUPS)), dma((NQ, 2, GROUPS)), dma((NX, 2, GROUPS)), dma, dma, dma,
            pltpu.SemaphoreType.REGULAR((6,)),
        ],
        compiler_params=pltpu.CompilerParams(
            collective_id=0, has_side_effects=True, vmem_limit_bytes=56 * 2**20
        ),
        name="swiglu_panel",
    )(gain.reshape(1, D), owner, lengths, dest.reshape(1, TOK), tokens, gate_weight, up_weight)


def solution(mesh):
    placed = (P("req", "own"), P(), P("req", "own"), P("req", "own"), P("req"), P("req"), P())
    return jax.shard_map(
        body,
        mesh=mesh,
        in_specs=placed,
        out_specs=(P("req", "own"), P("req", "own")),
        check_vma=False,
    )
```

```python
import functools

import jax
import jax.numpy as jnp
from jax import lax
from jax.experimental import pallas as pl
from jax.experimental.pallas import tpu as pltpu
from jax.sharding import PartitionSpec as P

MESH = pl.DeviceIdType.MESH
f32 = jnp.float32
bf16 = jnp.bfloat16

norm_eps = 1e-05
D = 16384
N_REQ = 64
N_OWN = 4
NX, NY, NZ = 4, 4, 8
TOK = 512
ROWS = 256
HID = 256
GROUPS = 2
PART = ROWS // GROUPS
PEERS = N_REQ // GROUPS
FEAT = 4096
PAIR = 4
NQ = 4
WC = 2 * HID
CUT = 160
CHAIN_T = (1, 3, 9, 11)
EDGE_T = (0, 4, 5, 9)
ORDER = (0, 3, 1, 2)
LAGS = (0, 4, 6, 10, 11)
RING_ON, RING_END, JOIN, GIVE_T, RELAY_T = 4, 8, 2, 8, 2
STREAM = 5 * NQ
LOAD_T = tuple(min(a, b) for a, b in zip(CHAIN_T, EDGE_T))
REST_T = [n for n in range(STREAM) if n not in CHAIN_T]
DOT_WAIT = (0, 0, 0, 0)
DOT_T = tuple(LAGS[4] + max(REST_T[4 * q + 3], CHAIN_T[q] + RING_END) + DOT_WAIT[q] for q in range(NQ))
TOTAL_T = [DOT_T[1] + 1]
for done in DOT_T[2:]:
    TOTAL_T.append(max(TOTAL_T[-1] + 1, done))
TOTAL_T.append(TOTAL_T[-1] + 1)


def kernel(
    gain, owner, lengths, dest, tok_hbm, gate_w, up_w,
    packed_out, local_hbm,
    tok, pick, act, act_out, panel, root_up, squares, squares_out, squares_in,
    part, part_out, part_in, red_out, red_in, hid, local_out, a2a_out, a2a_in, wide,
    s_tok, s_act, s_root_out, s_gate_in, s_up_in, s_sq_out, s_sq_in,
    s_chain_out, s_chain_in, s_ring_out, s_ring_in, s_edge_out, s_edge_in, s_spread_out, s_spread_in,
    s_part_out, s_part_in, s_red_out, s_red_in, s_a2a_out, s_a2a_in, s_local, relay,
):
    req = lax.axis_index("req")
    own = lax.axis_index("own")
    h, z, y = req // 32, (req // 4) % 8, req % 4
    j, c = own // 2, own % 2
    x = 2 * h + j

    def at(x_, y_, z_, c_):
        x_, y_, z_ = lax.rem(x_ + NX, NX), lax.rem(y_ + NY, NY), lax.rem(z_ + NZ, NZ)
        return ((x_ // 2 * NZ + z_) * NY + y_, (x_ % 2) * 2 + c_)

    def remote(src, dst, send, recv, device):
        return pltpu.make_async_remote_copy(
            src_ref=src, dst_ref=dst, send_sem=send, recv_sem=recv, device_id=device, device_id_type=MESH
        )

    def arrived(ref, sem):
        pltpu.make_async_copy(ref, ref, sem).wait()


    barrier = pltpu.get_barrier_semaphore()
    other_req = lax.rem(req + 32, N_REQ)
    beside = [at(x, y + 1, z, c), at(x, y - 1, z, c)], [at(x, y, z + 1, c), at(x, y, z - 1, c)]
    line = [(req, lax.rem(own + k, N_OWN)) for k in range(1, N_OWN)]
    line += [(other_req, lax.rem(own + k, N_OWN)) for k in range(N_OWN)]
    for device in line + beside[0] + beside[1]:
        pl.semaphore_signal(barrier, inc=1, device_id=device, device_id_type=MESH)

    fetch = pltpu.make_async_copy(tok_hbm, tok, s_tok)
    fetch.start()
    pl.semaphore_wait(barrier, 11)

    def pass_word(i):
        if i > 0:
            pl.semaphore_wait(relay.at[i - 1], 2)
        if i < 6:
            for device in beside[0 if i < 2 else 1]:
                pl.semaphore_signal(relay.at[i], inc=1, device_id=device, device_id_type=MESH)

    root = at(2 * (z % 2) + h, y, z, z // 4)
    self_root = jnp.logical_and(2 * (z % 2) + h == x, z // 4 == c)
    is_root = jnp.logical_and(z % 2 == h, z // 4 == c)
    zr = (z % 4) // 2

    def gate_at(k):
        return panel.at[k // 2, zr, y, :, pl.ds(pl.multiple_of(k % 2 * HID, HID), HID)]

    def to_root(src, dst, out, into):
        @pl.when(self_root)
        def _():
            pltpu.make_async_copy(src, dst, into).start()

        @pl.when(jnp.logical_not(self_root))
        def _():
            remote(src, dst, out, into, root).start()

    def gates_to_root():
        to_root(gate_w, gate_at(own), s_root_out.at[0], s_gate_in.at[own])

    def ups_to_root():
        to_root(up_w, root_up.at[own], s_root_out.at[1], s_up_in.at[own])

    gates_to_root()

    pass_word(0)

    slot = lax.broadcasted_iota(jnp.int32, (1, TOK), 1)
    span = jnp.where(
        slot < 128, lengths[0], jnp.where(slot < 256, lengths[1], jnp.where(slot < 384, lengths[2], lengths[3]))
    )
    live = (slot % 128) < span
    to = jnp.where(live, dest[...], -1)
    marks = (lax.broadcasted_iota(jnp.int32, (N_REQ, TOK), 0) == to).astype(f32)
    earlier = lax.broadcasted_iota(jnp.int32, (TOK, TOK), 0) < lax.broadcasted_iota(jnp.int32, (TOK, TOK), 1)
    before = jnp.dot(marks.astype(bf16), earlier.astype(f32).astype(bf16), preferred_element_type=f32)
    rank = jnp.sum(before * marks, axis=0, keepdims=True)
    row = jnp.where(live, rank * PEERS + (to // PEERS * PART + to % PEERS).astype(f32), -1.0)
    pick[...] = (lax.broadcasted_iota(jnp.int32, (ROWS, TOK), 0).astype(f32) == row).astype(f32).astype(bf16)
    fetch.wait()

    mine = pl.ds(pl.multiple_of(h * ROWS, ROWS), ROWS)

    def arrange(block, out):
        col = pl.multiple_of(block * 1024, 1024)
        rows = jnp.dot(pick[...], tok[:, pl.ds(col, 1024)], preferred_element_type=f32)
        sq = rows * rows
        for k in range(8):
            squares[...] += sq[:, k * 128 : (k + 1) * 128]
        out[...] = rows.astype(bf16)

    squares[...] = jnp.zeros_like(squares)
    for zz in range(2):
        arrange(1 - h + 2 * zz, act_out.at[:, pl.ds(zz * 1024, 1024)])
    for zz in range(2):
        arrange(h + 2 * zz, act.at[mine, pl.ds(zz * 1024, 1024)])

    partner = (other_req, own)
    give = remote(act_out, act.at[mine], s_act.at[0], s_act.at[1], partner)

    def turned(a, axis):
        eye = lax.broadcasted_iota(jnp.int32, (ROWS, ROWS), 0) == lax.broadcasted_iota(jnp.int32, (ROWS, ROWS), 1)
        return jnp.sum(jnp.where(eye, a, 0.0), axis=axis, keepdims=True)

    row_sums = turned(jnp.sum(squares[...], axis=1, keepdims=True), 0)
    squares_out[...] = jnp.broadcast_to(row_sums, (8, ROWS))
    sq_sends = []
    for k, device in enumerate(line):
        cp = remote(squares_out, squares_in.at[2 * own + h], s_sq_out.at[k], s_sq_in.at[2 * own + h], device)
        cp.start()
        sq_sends.append(cp)
    squares_in[2 * own + h] = squares_out[...]

    def normalize(hh):
        sums = squares_in[hh, 0:1, :]
        for k in range(1, N_OWN):
            sums = sums + squares_in[2 * k + hh, 0:1, :]
        scale = lax.rsqrt(turned(sums, 1) * (1.0 / D) + norm_eps)
        rows = pl.ds(pl.multiple_of(hh * ROWS, ROWS), ROWS)
        for zz in range(2):
            for n in range(2):
                cols = pl.ds(zz * 1024 + n * 512, 512)
                here = pl.multiple_of(own * FEAT + (h + 2 * zz) * 1024 + n * 512, 512)
                act[rows, cols] = (act[rows, cols].astype(f32) * scale * gain[:, pl.ds(here, 512)]).astype(bf16)

    def block(q, zz, yy, rows):
        return panel.at[q, zz, yy, pl.ds(rows[0], rows[1])]

    ra, rb = (0, CUT), (CUT, ROWS - CUT)

    def z_next(way):
        return at(x, y, z + 1 - 2 * way, c)

    def chain_copy(q, zz, way):
        ref = block(q, zz, y, ra)
        return remote(ref, ref, s_chain_out.at[q, zz, way], s_chain_in.at[q, zz], z_next(way))

    def spread_copy(q, zz, k, way):
        ref = block(q, zz, lax.rem(y + k, NY), rb)
        return remote(ref, ref, s_spread_out.at[q, zz, k, way], s_spread_in.at[q, zz, k], z_next(way))

    def y_copy(q, zz, k, rows, out, into, turn):
        way = turn if k == 2 else k
        yy = lax.rem(y + 3 - 2 * way, NY) if k == 2 else y
        ref = block(q, zz, yy, rows)
        return remote(ref, ref, out, into, at(x, y + 1 - 2 * way, z, c))

    def ring_copy(q, zz, k):
        return y_copy(q, zz, k, ra, s_ring_out.at[q, zz, k], s_ring_in.at[q, zz, k], zz)

    def edge_copy(q, k):
        return y_copy(q, zr, k, rb, s_edge_out.at[q, k], s_edge_in.at[q, k], lax.rem(q, 2))

    def y_arrived(q, zz, k, rows, into, turn):
        step = 2 if k == 2 else 3 - 2 * k
        arrived(block(q, zz, lax.rem(y + step, NY), rows), into)

    def reach(q, zz):
        d = lax.rem(z - (4 * c + h + 2 * zz) + 2 * NZ, NZ)
        far = 4 - lax.rem(q + zz, 2)
        return d, jnp.logical_and(d > 0, d < far), d >= far + 2

    def hops(zz):
        d = lax.rem(z - (4 * c + h + 2 * zz) + 2 * NZ, NZ)
        return jnp.minimum(d, NZ - d)

    def load_panel(q):
        @pl.when(q < 2)
        def _():
            for k in range(2):
                arrived(gate_at(2 * q + k), s_gate_in.at[2 * q + k])

        @pl.when(q == 2)
        def _():
            for k in range(N_OWN):
                arrived(root_up.at[k], s_up_in.at[k])

        @pl.when(q >= 2)
        def _():
            for k in range(2):
                stored = jnp.int32(0)
                for m in range(1, N_OWN):
                    stored = jnp.where(owner[m] == 2 * (q - 2) + k, m, stored)
                panel[q, zr, y, :, k * HID : (k + 1) * HID] = root_up[stored]

    def open_edges(q):
        for k in range(2):
            edge_copy(q, k).start()

    def on_chain(q, zz):
        d, up, down = reach(q, zz)

        @pl.when(d == 0)
        def _():
            for way in range(2):
                chain_copy(q, zz, way).start()

        @pl.when(d > 0)
        def _():
            arrived(block(q, zz, y, ra), s_chain_in.at[q, zz])

            @pl.when(jnp.logical_or(up, down))
            def _():
                chain_copy(q, zz, down.astype(jnp.int32)).start()

        for k in range(2):
            ring_copy(q, zz, k).start()

    def on_spread(q, zz, i):
        k = pick_from(ORDER, i)
        d, up, down = reach(q, zz)

        @pl.when(d == 0)
        def _():
            @pl.when(k > 0)
            def _():
                e = jnp.where(k == 3, 0, k)
                arrived(block(q, zz, lax.rem(y + k, NY), rb), s_edge_in.at[q, e])

                @pl.when(e == lax.rem(q, 2))
                def _():
                    edge_copy(q, 2).start()

            for way in range(2):
                spread_copy(q, zz, k, way).start()

        @pl.when(d > 0)
        def _():
            arrived(block(q, zz, lax.rem(y + k, NY), rb), s_spread_in.at[q, zz, k])

            @pl.when(jnp.logical_or(up, down))
            def _():
                spread_copy(q, zz, k, down.astype(jnp.int32)).start()

    def pick_from(table, i):
        out = jnp.int32(table[0])
        for k in range(1, len(table)):
            out = jnp.where(i >= k, table[k], out)
        return out

    def which(n, table):
        n_before, hit = jnp.int32(0), n == table[0]
        for v in table:
            n_before = n_before + (n > v).astype(jnp.int32)
            hit = jnp.logical_or(hit, n == v)
        return n_before, hit

    def flow(n, zz):
        @pl.when(jnp.logical_and(n >= 0, n < STREAM))
        def _():
            @pl.when(jnp.logical_and(is_root, zr == zz))
            def _():
                for table, f in ((LOAD_T, load_panel), (EDGE_T, open_edges)):
                    q, hit = which(n, table)

                    @pl.when(hit)
                    def _():
                        f(q)

            q, hit = which(n, CHAIN_T)

            @pl.when(hit)
            def _():
                on_chain(q, zz)

            @pl.when(jnp.logical_not(hit))
            def _():
                on_spread((n - q) // 4, zz, lax.rem(n - q, 4))

    def each_chunk(n, table, f):
        q, hit = which(n, table)

        @pl.when(hit)
        def _():
            f(q)

    def ring_on(zz, q):
        y_arrived(q, zz, zz, ra, s_ring_in.at[q, zz, zz], zz)
        ring_copy(q, zz, 2).start()

    def ring_end(zz, q):
        y_arrived(q, zz, 1 - zz, ra, s_ring_in.at[q, zz, 1 - zz], zz)
        y_arrived(q, zz, 2, ra, s_ring_in.at[q, zz, 2], zz)

    def part_copy(q, k, g):
        rows = pl.ds(g * PART, PART)
        return remote(
            part_out.at[q, k, rows], part_in.at[q, k, rows],
            s_part_out.at[q, k, g], s_part_in.at[q, k, g], (req, 2 * j + 1 - c),
        )

    def dot(q):
        for k in range(2):
            w = panel[q, :, :, :, k * HID : (k + 1) * HID].reshape(8 * ROWS, HID)
            part[q, k] = jnp.dot(act[...], w, preferred_element_type=f32)
            there = pl.ds(pl.multiple_of((1 - c) * ROWS, ROWS), ROWS)
            part_out[q, k] = part[q, k, there].astype(bf16)
            for g in range(GROUPS):
                part_copy(q, k, g).start()

    def red_copy(q, k, g):
        device = at(2 * c + lax.rem(q, 2), y, z, k)
        rows = pl.ds(g * PART, PART)
        return remote(
            red_out.at[q, k, rows], red_in.at[x, q // 2, rows],
            s_red_out.at[q, k, g], s_red_in.at[x, q // 2, g], device,
        )

    def red_here(q, k):
        return jnp.logical_and(2 * c + lax.rem(q, 2) == x, c == k)

    def total(q):
        for g in range(GROUPS):
            rows = pl.ds(g * PART, PART)
            mine_g = pl.ds(pl.multiple_of(c * ROWS + g * PART, PART), PART)
            for k in range(2):
                arrived(part_in.at[q, k, rows], s_part_in.at[q, k, g])
                both = (part[q, k, mine_g] + part_in[q, k, rows].astype(f32)).astype(bf16)
                here = red_here(q, k)

                @pl.when(here)
                def _():
                    red_in[x, q // 2, rows] = both

                @pl.when(jnp.logical_not(here))
                def _():
                    red_out[q, k, rows] = both
                    red_copy(q, k, g).start()

    def left(q):
        for zz in range(2):
            d, up, down = reach(q, zz)
            for way, on in enumerate((up, down)):
                @pl.when(jnp.logical_or(d == 0, on))
                def _():
                    chain_copy(q, zz, way).wait_send()
                    for k in range(NY):
                        spread_copy(q, zz, k, way).wait_send()
            for k in range(3):
                ring_copy(q, zz, k).wait_send()

        @pl.when(is_root)
        def _():
            for k in range(3):
                edge_copy(q, k).wait_send()

        for k in range(2):
            for g in range(GROUPS):
                part_copy(q, k, g).wait_send()

    first = (hops(1) < hops(0)).astype(jnp.int32)

    def once(t, when, f, *args):
        @pl.when(t == when)
        def _():
            f(*args)

    def normalize_given():
        give.wait_recv()
        normalize(1 - h)

    def normalize_mine():
        for k in range(1, 8):
            slot = lax.rem(2 * own + h + k, 8)
            arrived(squares_in.at[slot], s_sq_in.at[slot])
        normalize(h)

    behind = [pick_from(LAGS, hops(zz)) for zz in range(2)]
    near = jnp.minimum(behind[0], behind[1])

    ups_to_root()

    def turn(t, _):
        once(t, near + GIVE_T, give.start)
        for i in range(1, 7):
            once(t, i * RELAY_T, pass_word, i)

        for zz in (first, 1 - first):
            flow(t - jnp.where(zz == 0, behind[0], behind[1]), zz)
        for zz in range(2):
            each_chunk(t - behind[zz] - RING_ON, CHAIN_T, functools.partial(ring_on, zz))
        for zz in range(2):
            each_chunk(t - behind[zz] - RING_END, CHAIN_T, functools.partial(ring_end, zz))

        @pl.when(t == DOT_T[0] - 1)
        def _():
            normalize_mine()
            normalize_given()

        each_chunk(t, DOT_T, dot)
        each_chunk(t, TOTAL_T, total)
        each_chunk(t, TOTAL_T[:-1], left)
        return 0

    lax.fori_loop(0, TOTAL_T[-1] + 1, turn, 0)

    my_tile = pl.ds(pl.multiple_of(req * 8, 8), 8)

    def send_tile(to_req):
        src = a2a_out.at[pl.ds(pl.multiple_of(to_req * 8, 8), 8)]
        remote(src, a2a_in.at[my_tile], s_a2a_out, s_a2a_in, (to_req, own)).start()

    for g in range(GROUPS):
        rows = pl.ds(g * PART, PART)
        for k in range(NX):
            @pl.when(jnp.logical_or(x != k, h != c))
            def _():
                for kind in range(2):
                    arrived(red_in.at[k, kind, rows], s_red_in.at[k, kind, g])

        gate, up = red_in[0, 0, rows].astype(f32), red_in[0, 1, rows].astype(f32)
        for k in range(1, NX):
            gate = gate + red_in[k, 0, rows].astype(f32)
            up = up + red_in[k, 1, rows].astype(f32)
        hidden = (gate / (1.0 + jnp.exp(-gate)) * up).astype(bf16)
        hid[rows] = hidden
        hidden = hidden.astype(f32)
        for half in range(2):
            for k in range(PAIR):
                a2a_out[pl.ds(g * 8 * PEERS + half * PAIR + k, PEERS, stride=8), :] = hidden[
                    k * PEERS : (k + 1) * PEERS, half * 128 : (half + 1) * 128
                ]

        def send_near(i, _):
            send_tile(PEERS * g + lax.rem(req + i, PEERS))
            return 0

        lax.fori_loop(1, PEERS, send_near, 0)

        @pl.when(req // PEERS != g)
        def _():
            send_tile(PEERS * g + lax.rem(req, PEERS))

    local_out[...] = lax.dot_general(
        pick[...], hid[...], (((0,), (0,)), ((), ())), preferred_element_type=f32
    ).astype(bf16)
    keep_local = pltpu.make_async_copy(local_out, local_hbm, s_local)
    keep_local.start()
    a2a_in[my_tile, :] = a2a_out[my_tile, :]

    left(NQ - 1)
    for q in range(NQ):
        for k in range(2):
            @pl.when(jnp.logical_not(red_here(q, k)))
            def _():
                for g in range(GROUPS):
                    red_copy(q, k, g).wait_send()
    give.wait_send()
    for cp in sq_sends:
        cp.wait_send()

    @pl.when(jnp.logical_not(self_root))
    def _():
        remote(gate_w, gate_at(own), s_root_out.at[0], s_gate_in.at[own], root).wait_send()
        remote(up_w, root_up.at[own], s_root_out.at[1], s_up_in.at[own], root).wait_send()

    others = pl.ds(0, 8 * (N_REQ - 1))
    arrived(a2a_out.at[others], s_a2a_out)
    arrived(a2a_in.at[others], s_a2a_in)
    for half in range(2):
        for k in range(PAIR):
            wide[pl.ds(k, N_REQ, stride=PAIR), :] = a2a_in[pl.ds(half * PAIR + k, N_REQ, stride=8), :]
        packed_out[:, half * 128 : (half + 1) * 128] = wide[...].astype(bf16)
    keep_local.wait()


def body(tokens, gain, gate_weight, up_weight, lengths, dest, owner):
    vmem = pl.BlockSpec(memory_space=pltpu.VMEM)
    smem = pl.BlockSpec(memory_space=pltpu.SMEM)
    dma = pltpu.SemaphoreType.DMA
    return pl.pallas_call(
        kernel,
        out_shape=(jax.ShapeDtypeStruct((ROWS, HID), bf16), jax.ShapeDtypeStruct((TOK, HID), bf16)),
        in_specs=[vmem, smem, smem, vmem, pl.BlockSpec(memory_space=pl.ANY), vmem, vmem],
        out_specs=(vmem, pl.BlockSpec(memory_space=pl.ANY)),
        scratch_shapes=[
            pltpu.VMEM((TOK, FEAT), bf16),
            pltpu.VMEM((ROWS, TOK), bf16),
            pltpu.VMEM((2 * ROWS, FEAT // 2), bf16),
            pltpu.VMEM((ROWS, FEAT // 2), bf16),
            pltpu.VMEM((NQ, 2, NY, ROWS, WC), bf16),
            pltpu.VMEM((N_OWN, ROWS, HID), bf16),
            pltpu.VMEM((ROWS, 128), f32),
            pltpu.VMEM((8, ROWS), f32),
            pltpu.VMEM((8, 8, ROWS), f32),
            pltpu.VMEM((NQ, 2, 2 * ROWS, HID), f32),
            pltpu.VMEM((NQ, 2, ROWS, HID), bf16),
            pltpu.VMEM((NQ, 2, ROWS, HID), bf16),
            pltpu.VMEM((NQ, 2, ROWS, HID), bf16),
            pltpu.VMEM((NX, 2, ROWS, HID), bf16),
            pltpu.VMEM((ROWS, HID), bf16),
            pltpu.VMEM((TOK, HID), bf16),
            pltpu.VMEM((8 * N_REQ, 128), f32),
            pltpu.VMEM((8 * N_REQ, 128), f32),
            pltpu.VMEM((ROWS, 128), f32),
            dma, dma((2,)), dma((2,)), dma((N_OWN,)), dma((N_OWN,)), dma((7,)), dma((8,)),
            dma((NQ, 2, 2)), dma((NQ, 2)), dma((NQ, 2, 3)), dma((NQ, 2, 3)), dma((NQ, 3)), dma((NQ, 3)),
            dma((NQ, 2, NY, 2)), dma((NQ, 2, NY)),
            dma((NQ, 2, GROUPS)), dma((NQ, 2, GROUPS)), dma((NQ, 2, GROUPS)), dma((NX, 2, GROUPS)), dma, dma, dma,
            pltpu.SemaphoreType.REGULAR((6,)),
        ],
        compiler_params=pltpu.CompilerParams(
            collective_id=0, has_side_effects=True, vmem_limit_bytes=56 * 2**20
        ),
        name="swiglu_panel",
    )(gain.reshape(1, D), owner, lengths, dest.reshape(1, TOK), tokens, gate_weight, up_weight)


def solution(mesh):
    placed = (P("req", "own"), P(), P("req", "own"), P("req", "own"), P("req"), P("req"), P())
    return jax.shard_map(
        body,
        mesh=mesh,
        in_specs=placed,
        out_specs=(P("req", "own"), P("req", "own")),
        check_vma=False,
    )
```

```python
import functools

import jax
import jax.numpy as jnp
from jax import lax
from jax.experimental import pallas as pl
from jax.experimental.pallas import tpu as pltpu
from jax.sharding import PartitionSpec as P

MESH = pl.DeviceIdType.MESH
f32 = jnp.float32
bf16 = jnp.bfloat16

norm_eps = 1e-05
D = 16384
N_REQ = 64
N_OWN = 4
NX, NY, NZ = 4, 4, 8
TOK = 512
ROWS = 256
HID = 256
GROUPS = 2
PART = ROWS // GROUPS
PEERS = N_REQ // GROUPS
FEAT = 4096
PAIR = 4
NQ = 4
WC = 2 * HID
CUT = 160
CHAIN_T = (1, 3, 9, 11)
EDGE_T = (0, 4, 5, 9)
ORDER = (0, 3, 1, 2)
LAGS = (0, 4, 6, 10, 11)
RING_ON, RING_END, JOIN, GIVE_T, RELAY_T = 4, 8, 2, 7, 2
STREAM = 5 * NQ
LOAD_T = tuple(min(a, b) for a, b in zip(CHAIN_T, EDGE_T))
REST_T = [n for n in range(STREAM) if n not in CHAIN_T]
DOT_WAIT = (0, 0, 0, 0)
DOT_T = tuple(LAGS[4] + max(REST_T[4 * q + 3], CHAIN_T[q] + RING_END) + DOT_WAIT[q] for q in range(NQ))
TOTAL_T = [DOT_T[1] + 1]
for done in DOT_T[2:]:
    TOTAL_T.append(max(TOTAL_T[-1] + 1, done))
TOTAL_T.append(TOTAL_T[-1] + 1)


def kernel(
    gain, owner, lengths, dest, tok_hbm, gate_w, up_w,
    packed_out, local_hbm,
    tok, pick, act, act_out, panel, root_up, squares, squares_out, squares_in,
    part, part_in, red_out, red_in, hid, local_out, a2a_out, a2a_in, wide,
    s_tok, s_act, s_root_out, s_gate_in, s_up_in, s_sq_out, s_sq_in,
    s_chain_out, s_chain_in, s_ring_out, s_ring_in, s_edge_out, s_edge_in, s_spread_out, s_spread_in,
    s_part_out, s_part_in, s_red_out, s_red_in, s_a2a_out, s_a2a_in, s_local, relay,
):
    req = lax.axis_index("req")
    own = lax.axis_index("own")
    h, z, y = req // 32, (req // 4) % 8, req % 4
    j, c = own // 2, own % 2
    x = 2 * h + j

    def at(x_, y_, z_, c_):
        x_, y_, z_ = lax.rem(x_ + NX, NX), lax.rem(y_ + NY, NY), lax.rem(z_ + NZ, NZ)
        return ((x_ // 2 * NZ + z_) * NY + y_, (x_ % 2) * 2 + c_)

    def remote(src, dst, send, recv, device):
        return pltpu.make_async_remote_copy(
            src_ref=src, dst_ref=dst, send_sem=send, recv_sem=recv, device_id=device, device_id_type=MESH
        )

    def arrived(ref, sem):
        pltpu.make_async_copy(ref, ref, sem).wait()


    barrier = pltpu.get_barrier_semaphore()
    other_req = lax.rem(req + 32, N_REQ)
    beside = [at(x, y + 1, z, c), at(x, y - 1, z, c)], [at(x, y, z + 1, c), at(x, y, z - 1, c)]
    line = [(req, lax.rem(own + k, N_OWN)) for k in range(1, N_OWN)]
    line += [(other_req, lax.rem(own + k, N_OWN)) for k in range(N_OWN)]
    for device in line + beside[0] + beside[1]:
        pl.semaphore_signal(barrier, inc=1, device_id=device, device_id_type=MESH)

    fetch = pltpu.make_async_copy(tok_hbm, tok, s_tok)
    fetch.start()
    pl.semaphore_wait(barrier, 11)

    def pass_word(i):
        if i > 0:
            pl.semaphore_wait(relay.at[i - 1], 2)
        if i < 6:
            for device in beside[0 if i < 2 else 1]:
                pl.semaphore_signal(relay.at[i], inc=1, device_id=device, device_id_type=MESH)

    root = at(2 * (z % 2) + h, y, z, z // 4)
    self_root = jnp.logical_and(2 * (z % 2) + h == x, z // 4 == c)
    is_root = jnp.logical_and(z % 2 == h, z // 4 == c)
    zr = (z % 4) // 2

    def gate_at(k):
        return panel.at[k // 2, zr, y, :, pl.ds(pl.multiple_of(k % 2 * HID, HID), HID)]

    def to_root(src, dst, out, into):
        @pl.when(self_root)
        def _():
            pltpu.make_async_copy(src, dst, into).start()

        @pl.when(jnp.logical_not(self_root))
        def _():
            remote(src, dst, out, into, root).start()

    def gates_to_root():
        to_root(gate_w, gate_at(own), s_root_out.at[0], s_gate_in.at[own])

    def ups_to_root():
        to_root(up_w, root_up.at[own], s_root_out.at[1], s_up_in.at[own])

    gates_to_root()

    pass_word(0)

    slot = lax.broadcasted_iota(jnp.int32, (1, TOK), 1)
    span = jnp.where(
        slot < 128, lengths[0], jnp.where(slot < 256, lengths[1], jnp.where(slot < 384, lengths[2], lengths[3]))
    )
    live = (slot % 128) < span
    to = jnp.where(live, dest[...], -1)
    marks = (lax.broadcasted_iota(jnp.int32, (N_REQ, TOK), 0) == to).astype(f32)
    earlier = lax.broadcasted_iota(jnp.int32, (TOK, TOK), 0) < lax.broadcasted_iota(jnp.int32, (TOK, TOK), 1)
    before = jnp.dot(marks.astype(bf16), earlier.astype(f32).astype(bf16), preferred_element_type=f32)
    rank = jnp.sum(before * marks, axis=0, keepdims=True)
    row = jnp.where(live, rank * PEERS + (to // PEERS * PART + to % PEERS).astype(f32), -1.0)
    pick[...] = (lax.broadcasted_iota(jnp.int32, (ROWS, TOK), 0).astype(f32) == row).astype(f32).astype(bf16)
    fetch.wait()

    mine = pl.ds(pl.multiple_of(h * ROWS, ROWS), ROWS)

    def arrange(block, out):
        col = pl.multiple_of(block * 1024, 1024)
        rows = jnp.dot(pick[...], tok[:, pl.ds(col, 1024)], preferred_element_type=f32)
        sq = rows * rows
        for k in range(8):
            squares[...] += sq[:, k * 128 : (k + 1) * 128]
        out[...] = rows.astype(bf16)

    squares[...] = jnp.zeros_like(squares)
    for zz in range(2):
        arrange(1 - h + 2 * zz, act_out.at[:, pl.ds(zz * 1024, 1024)])
    for zz in range(2):
        arrange(h + 2 * zz, act.at[mine, pl.ds(zz * 1024, 1024)])

    partner = (other_req, own)
    give = remote(act_out, act.at[mine], s_act.at[0], s_act.at[1], partner)

    def turned(a, axis):
        eye = lax.broadcasted_iota(jnp.int32, (ROWS, ROWS), 0) == lax.broadcasted_iota(jnp.int32, (ROWS, ROWS), 1)
        return jnp.sum(jnp.where(eye, a, 0.0), axis=axis, keepdims=True)

    row_sums = turned(jnp.sum(squares[...], axis=1, keepdims=True), 0)
    squares_out[...] = jnp.broadcast_to(row_sums, (8, ROWS))
    sq_sends = []
    for k, device in enumerate(line):
        cp = remote(squares_out, squares_in.at[2 * own + h], s_sq_out.at[k], s_sq_in.at[2 * own + h], device)
        cp.start()
        sq_sends.append(cp)
    squares_in[2 * own + h] = squares_out[...]

    def normalize(hh):
        sums = squares_in[hh, 0:1, :]
        for k in range(1, N_OWN):
            sums = sums + squares_in[2 * k + hh, 0:1, :]
        scale = lax.rsqrt(turned(sums, 1) * (1.0 / D) + norm_eps)
        rows = pl.ds(pl.multiple_of(hh * ROWS, ROWS), ROWS)
        for zz in range(2):
            for n in range(2):
                cols = pl.ds(zz * 1024 + n * 512, 512)
                here = pl.multiple_of(own * FEAT + (h + 2 * zz) * 1024 + n * 512, 512)
                act[rows, cols] = (act[rows, cols].astype(f32) * scale * gain[:, pl.ds(here, 512)]).astype(bf16)

    def block(q, zz, yy, rows):
        return panel.at[q, zz, yy, pl.ds(rows[0], rows[1])]

    ra, rb = (0, CUT), (CUT, ROWS - CUT)

    def z_next(way):
        return at(x, y, z + 1 - 2 * way, c)

    def chain_copy(q, zz, way):
        ref = block(q, zz, y, ra)
        return remote(ref, ref, s_chain_out.at[q, zz, way], s_chain_in.at[q, zz], z_next(way))

    def spread_copy(q, zz, k, way):
        ref = block(q, zz, lax.rem(y + k, NY), rb)
        return remote(ref, ref, s_spread_out.at[q, zz, k, way], s_spread_in.at[q, zz, k], z_next(way))

    def y_copy(q, zz, k, rows, out, into, turn):
        way = turn if k == 2 else k
        yy = lax.rem(y + 3 - 2 * way, NY) if k == 2 else y
        ref = block(q, zz, yy, rows)
        return remote(ref, ref, out, into, at(x, y + 1 - 2 * way, z, c))

    def ring_copy(q, zz, k):
        return y_copy(q, zz, k, ra, s_ring_out.at[q, zz, k], s_ring_in.at[q, zz, k], zz)

    def edge_copy(q, k):
        return y_copy(q, zr, k, rb, s_edge_out.at[q, k], s_edge_in.at[q, k], lax.rem(q, 2))

    def y_arrived(q, zz, k, rows, into, turn):
        step = 2 if k == 2 else 3 - 2 * k
        arrived(block(q, zz, lax.rem(y + step, NY), rows), into)

    def reach(q, zz):
        d = lax.rem(z - (4 * c + h + 2 * zz) + 2 * NZ, NZ)
        far = 4 - lax.rem(q + zz, 2)
        return d, jnp.logical_and(d > 0, d < far), d >= far + 2

    def hops(zz):
        d = lax.rem(z - (4 * c + h + 2 * zz) + 2 * NZ, NZ)
        return jnp.minimum(d, NZ - d)

    def load_panel(q):
        @pl.when(q < 2)
        def _():
            for k in range(2):
                arrived(gate_at(2 * q + k), s_gate_in.at[2 * q + k])

        @pl.when(q == 2)
        def _():
            for k in range(N_OWN):
                arrived(root_up.at[k], s_up_in.at[k])

        @pl.when(q >= 2)
        def _():
            for k in range(2):
                stored = jnp.int32(0)
                for m in range(1, N_OWN):
                    stored = jnp.where(owner[m] == 2 * (q - 2) + k, m, stored)
                panel[q, zr, y, :, k * HID : (k + 1) * HID] = root_up[stored]

    def open_edges(q):
        for k in range(2):
            edge_copy(q, k).start()

    def on_chain(q, zz):
        d, up, down = reach(q, zz)

        @pl.when(d == 0)
        def _():
            for way in range(2):
                chain_copy(q, zz, way).start()

        @pl.when(d > 0)
        def _():
            arrived(block(q, zz, y, ra), s_chain_in.at[q, zz])

            @pl.when(jnp.logical_or(up, down))
            def _():
                chain_copy(q, zz, down.astype(jnp.int32)).start()

        for k in range(2):
            ring_copy(q, zz, k).start()

    def on_spread(q, zz, i):
        k = pick_from(ORDER, i)
        d, up, down = reach(q, zz)

        @pl.when(d == 0)
        def _():
            @pl.when(k > 0)
            def _():
                e = jnp.where(k == 3, 0, k)
                arrived(block(q, zz, lax.rem(y + k, NY), rb), s_edge_in.at[q, e])

                @pl.when(e == lax.rem(q, 2))
                def _():
                    edge_copy(q, 2).start()

            for way in range(2):
                spread_copy(q, zz, k, way).start()

        @pl.when(d > 0)
        def _():
            arrived(block(q, zz, lax.rem(y + k, NY), rb), s_spread_in.at[q, zz, k])

            @pl.when(jnp.logical_or(up, down))
            def _():
                spread_copy(q, zz, k, down.astype(jnp.int32)).start()

    def pick_from(table, i):
        out = jnp.int32(table[0])
        for k in range(1, len(table)):
            out = jnp.where(i >= k, table[k], out)
        return out

    def which(n, table):
        n_before, hit = jnp.int32(0), n == table[0]
        for v in table:
            n_before = n_before + (n > v).astype(jnp.int32)
            hit = jnp.logical_or(hit, n == v)
        return n_before, hit

    def flow(n, zz):
        @pl.when(jnp.logical_and(n >= 0, n < STREAM))
        def _():
            @pl.when(jnp.logical_and(is_root, zr == zz))
            def _():
                for table, f in ((LOAD_T, load_panel), (EDGE_T, open_edges)):
                    q, hit = which(n, table)

                    @pl.when(hit)
                    def _():
                        f(q)

            q, hit = which(n, CHAIN_T)

            @pl.when(hit)
            def _():
                on_chain(q, zz)

            @pl.when(jnp.logical_not(hit))
            def _():
                on_spread((n - q) // 4, zz, lax.rem(n - q, 4))

    def each_chunk(n, table, f):
        q, hit = which(n, table)

        @pl.when(hit)
        def _():
            f(q)

    def ring_on(zz, q):
        y_arrived(q, zz, zz, ra, s_ring_in.at[q, zz, zz], zz)
        ring_copy(q, zz, 2).start()

    def ring_end(zz, q):
        y_arrived(q, zz, 1 - zz, ra, s_ring_in.at[q, zz, 1 - zz], zz)
        y_arrived(q, zz, 2, ra, s_ring_in.at[q, zz, 2], zz)

    def part_copy(q, k, g):
        here, there = pl.ds(pl.multiple_of((1 - c) * ROWS + g * PART, PART), PART), pl.ds(g * PART, PART)
        return remote(
            part.at[q, k, here], part_in.at[q, k, there],
            s_part_out.at[q, k, g], s_part_in.at[q, k, g], (req, 2 * j + 1 - c),
        )

    def dot(q):
        for k in range(2):
            w = panel[q, :, :, :, k * HID : (k + 1) * HID].reshape(8 * ROWS, HID)
            part[q, k] = jnp.dot(act[...], w, preferred_element_type=f32)
            for g in range(GROUPS):
                part_copy(q, k, g).start()

    def red_copy(q, k, g):
        device = at(2 * c + lax.rem(q, 2), y, z, k)
        rows = pl.ds(g * PART, PART)
        return remote(
            red_out.at[q, k, rows], red_in.at[x, q // 2, rows],
            s_red_out.at[q, k, g], s_red_in.at[x, q // 2, g], device,
        )

    def red_here(q, k):
        return jnp.logical_and(2 * c + lax.rem(q, 2) == x, c == k)

    def total(q):
        for g in range(GROUPS):
            rows = pl.ds(g * PART, PART)
            mine_g = pl.ds(pl.multiple_of(c * ROWS + g * PART, PART), PART)
            for k in range(2):
                arrived(part_in.at[q, k, rows], s_part_in.at[q, k, g])
                both = (part[q, k, mine_g] + part_in[q, k, rows]).astype(bf16)
                here = red_here(q, k)

                @pl.when(here)
                def _():
                    red_in[x, q // 2, rows] = both

                @pl.when(jnp.logical_not(here))
                def _():
                    red_out[q, k, rows] = both
                    red_copy(q, k, g).start()

    def left(q):
        for zz in range(2):
            d, up, down = reach(q, zz)
            for way, on in enumerate((up, down)):
                @pl.when(jnp.logical_or(d == 0, on))
                def _():
                    chain_copy(q, zz, way).wait_send()
                    for k in range(NY):
                        spread_copy(q, zz, k, way).wait_send()
            for k in range(3):
                ring_copy(q, zz, k).wait_send()

        @pl.when(is_root)
        def _():
            for k in range(3):
                edge_copy(q, k).wait_send()

        for k in range(2):
            for g in range(GROUPS):
                part_copy(q, k, g).wait_send()

    first = (hops(1) < hops(0)).astype(jnp.int32)

    def once(t, when, f, *args):
        @pl.when(t == when)
        def _():
            f(*args)

    def normalize_given():
        give.wait_recv()
        normalize(1 - h)

    def normalize_mine():
        for k in range(1, 8):
            slot = lax.rem(2 * own + h + k, 8)
            arrived(squares_in.at[slot], s_sq_in.at[slot])
        normalize(h)

    behind = [pick_from(LAGS, hops(zz)) for zz in range(2)]
    near = jnp.minimum(behind[0], behind[1])

    ups_to_root()

    def turn(t, _):
        once(t, near + GIVE_T, give.start)
        once(t, near + GIVE_T - 2, normalize_mine)
        for i in range(1, 7):
            once(t, i * RELAY_T, pass_word, i)

        for zz in (first, 1 - first):
            flow(t - jnp.where(zz == 0, behind[0], behind[1]), zz)
        for zz in range(2):
            each_chunk(t - behind[zz] - RING_ON, CHAIN_T, functools.partial(ring_on, zz))
        for zz in range(2):
            each_chunk(t - behind[zz] - RING_END, CHAIN_T, functools.partial(ring_end, zz))

        @pl.when(t == DOT_T[0] - 1)
        def _():
            normalize_given()

        each_chunk(t, DOT_T, dot)
        each_chunk(t, TOTAL_T, total)
        each_chunk(t, TOTAL_T[:-1], left)
        return 0

    lax.fori_loop(0, TOTAL_T[-1] + 1, turn, 0)

    my_tile = pl.ds(pl.multiple_of(req * 8, 8), 8)

    def send_tile(to_req):
        src = a2a_out.at[pl.ds(pl.multiple_of(to_req * 8, 8), 8)]
        remote(src, a2a_in.at[my_tile], s_a2a_out, s_a2a_in, (to_req, own)).start()

    for g in range(GROUPS):
        rows = pl.ds(g * PART, PART)
        for k in range(NX):
            @pl.when(jnp.logical_or(x != k, h != c))
            def _():
                for kind in range(2):
                    arrived(red_in.at[k, kind, rows], s_red_in.at[k, kind, g])

        gate, up = red_in[0, 0, rows].astype(f32), red_in[0, 1, rows].astype(f32)
        for k in range(1, NX):
            gate = gate + red_in[k, 0, rows].astype(f32)
            up = up + red_in[k, 1, rows].astype(f32)
        hidden = (gate / (1.0 + jnp.exp(-gate)) * up).astype(bf16)
        hid[rows] = hidden
        hidden = hidden.astype(f32)
        for half in range(2):
            for k in range(PAIR):
                a2a_out[pl.ds(g * 8 * PEERS + half * PAIR + k, PEERS, stride=8), :] = hidden[
                    k * PEERS : (k + 1) * PEERS, half * 128 : (half + 1) * 128
                ]

        def send_near(i, _):
            send_tile(PEERS * g + lax.rem(req + i, PEERS))
            return 0

        lax.fori_loop(1, PEERS, send_near, 0)

        @pl.when(req // PEERS != g)
        def _():
            send_tile(PEERS * g + lax.rem(req, PEERS))

    local_out[...] = lax.dot_general(
        pick[...], hid[...], (((0,), (0,)), ((), ())), preferred_element_type=f32
    ).astype(bf16)
    keep_local = pltpu.make_async_copy(local_out, local_hbm, s_local)
    keep_local.start()
    a2a_in[my_tile, :] = a2a_out[my_tile, :]

    left(NQ - 1)
    for q in range(NQ):
        for k in range(2):
            @pl.when(jnp.logical_not(red_here(q, k)))
            def _():
                for g in range(GROUPS):
                    red_copy(q, k, g).wait_send()
    give.wait_send()
    for cp in sq_sends:
        cp.wait_send()

    @pl.when(jnp.logical_not(self_root))
    def _():
        remote(gate_w, gate_at(own), s_root_out.at[0], s_gate_in.at[own], root).wait_send()
        remote(up_w, root_up.at[own], s_root_out.at[1], s_up_in.at[own], root).wait_send()

    others = pl.ds(0, 8 * (N_REQ - 1))
    arrived(a2a_out.at[others], s_a2a_out)
    arrived(a2a_in.at[others], s_a2a_in)
    for half in range(2):
        for k in range(PAIR):
            wide[pl.ds(k, N_REQ, stride=PAIR), :] = a2a_in[pl.ds(half * PAIR + k, N_REQ, stride=8), :]
        packed_out[:, half * 128 : (half + 1) * 128] = wide[...].astype(bf16)
    keep_local.wait()


def body(tokens, gain, gate_weight, up_weight, lengths, dest, owner):
    vmem = pl.BlockSpec(memory_space=pltpu.VMEM)
    smem = pl.BlockSpec(memory_space=pltpu.SMEM)
    dma = pltpu.SemaphoreType.DMA
    return pl.pallas_call(
        kernel,
        out_shape=(jax.ShapeDtypeStruct((ROWS, HID), bf16), jax.ShapeDtypeStruct((TOK, HID), bf16)),
        in_specs=[vmem, smem, smem, vmem, pl.BlockSpec(memory_space=pl.ANY), vmem, vmem],
        out_specs=(vmem, pl.BlockSpec(memory_space=pl.ANY)),
        scratch_shapes=[
            pltpu.VMEM((TOK, FEAT), bf16),
            pltpu.VMEM((ROWS, TOK), bf16),
            pltpu.VMEM((2 * ROWS, FEAT // 2), bf16),
            pltpu.VMEM((ROWS, FEAT // 2), bf16),
            pltpu.VMEM((NQ, 2, NY, ROWS, WC), bf16),
            pltpu.VMEM((N_OWN, ROWS, HID), bf16),
            pltpu.VMEM((ROWS, 128), f32),
            pltpu.VMEM((8, ROWS), f32),
            pltpu.VMEM((8, 8, ROWS), f32),
            pltpu.VMEM((NQ, 2, 2 * ROWS, HID), f32),
            pltpu.VMEM((NQ, 2, ROWS, HID), f32),
            pltpu.VMEM((NQ, 2, ROWS, HID), bf16),
            pltpu.VMEM((NX, 2, ROWS, HID), bf16),
            pltpu.VMEM((ROWS, HID), bf16),
            pltpu.VMEM((TOK, HID), bf16),
            pltpu.VMEM((8 * N_REQ, 128), f32),
            pltpu.VMEM((8 * N_REQ, 128), f32),
            pltpu.VMEM((ROWS, 128), f32),
            dma, dma((2,)), dma((2,)), dma((N_OWN,)), dma((N_OWN,)), dma((7,)), dma((8,)),
            dma((NQ, 2, 2)), dma((NQ, 2)), dma((NQ, 2, 3)), dma((NQ, 2, 3)), dma((NQ, 3)), dma((NQ, 3)),
            dma((NQ, 2, NY, 2)), dma((NQ, 2, NY)),
            dma((NQ, 2, GROUPS)), dma((NQ, 2, GROUPS)), dma((NQ, 2, GROUPS)), dma((NX, 2, GROUPS)), dma, dma, dma,
            pltpu.SemaphoreType.REGULAR((6,)),
        ],
        compiler_params=pltpu.CompilerParams(
            collective_id=0, has_side_effects=True, vmem_limit_bytes=56 * 2**20
        ),
        name="swiglu_panel",
    )(gain.reshape(1, D), owner, lengths, dest.reshape(1, TOK), tokens, gate_weight, up_weight)


def solution(mesh):
    placed = (P("req", "own"), P(), P("req", "own"), P("req", "own"), P("req"), P("req"), P())
    return jax.shard_map(
        body,
        mesh=mesh,
        in_specs=placed,
        out_specs=(P("req", "own"), P("req", "own")),
        check_vma=False,
    )
```
